32 devices in a mesh: lat: 4 (over y, x), lon: 8 (over z, core).
Axes of the slice: x: 2, y: 2, z: 4, core: 2. Of those that a mesh axis runs over, the one named last changes fastest.
Arguments:
- feat_one: bfloat16 [64, 512, 256], P('lat', 'lon'), may hold values from -6 to 6
- feat_two: bfloat16 [64, 512, 256], P('lat', 'lon'), may hold values from -6 to 6
- context_in: bfloat16 [64, 512, 128], P('lat', 'lon'), may hold values from 0 to 2
- hidden_init: bfloat16 [64, 512, 128], P('lat', 'lon'), may hold values from -1 to 1
- corr_proj: bfloat16 [8, 128, 128], replicated, may hold values from -0.5 to 0.5
- input_conv: bfloat16 [2, 5, 256, 384], replicated, may hold values from -0.125 to 0.125
- state_zr: bfloat16 [2, 5, 128, 256], replicated, may hold values from -0.75 to 0.75
- state_q: bfloat16 [2, 5, 128, 128], replicated, may hold values from -0.75 to 0.75
- update_bias: float32 [2, 128], replicated, may hold values from -2 to 0
- gate_bias: float32 [2, 256], replicated, may hold values from -3 to 3
- blk_offset: int32 [4, 8, 12], P('lat', 'lon'), may hold values from -4 to 4, as said below
- blk_class: int32 [4, 8, 12], P('lat', 'lon'), may hold values from 0 to 7
- blk_count: int32 [4, 8], P('lat', 'lon'), may hold values from 1 to 12, as said below
Outputs:
- hidden: bfloat16 [64, 512, 128], P('lat', 'lon')
The draws below stay inside these ranges and needn't reach their ends.
Inputs may be any that keep to these rules, and one draw needn't show every extreme that they name: `blk_offset`: offsets of panels along the closed longitude loop; bands nearer a pole reach farther, the bands at the poles up to 4 either way, and both ends are reached in every draw. Slots at or beyond blk_count are unused. `blk_count`: bands nearer a pole hold more live slots; some panel of the first band holds 12.
All inputs are finite; a program needn't handle non-finite values.
Results may differ from the reference program's by a relative error of at most 0.019.
Values may be sent and summed in bfloat16 or wider, within the bound.
A program may use at most 64 MiB of HBM per device.

```python
import jax
import jax.numpy as jnp
from jax import lax

C = 256
H = 128
ROWS = 16
COLS = 64
POOLR = 8
POOLC = 16
MAXB = 12
RMAX = 4
NCLASS = 8
ITERS = 4
NLAT = 64
NLON = 512
N_LAT = 4
N_LON = 8


def forced_column(key):
    return jax.random.randint(jax.random.fold_in(key, 7), (), 0, N_LON)


def band_distance():
    latitude = jnp.arange(N_LAT, dtype=jnp.int32)
    return jnp.abs(2 * latitude + 1 - N_LAT)


def draw_blk_count(key, part):
    distance = band_distance()
    denom = max((N_LAT - 1) ** 2, 1)
    top = 2 + (MAXB - 2) * distance * distance // denom
    lowest = jnp.maximum(top - 2, 1)
    extra = jax.random.randint(jax.random.fold_in(key, 1), (N_LAT, N_LON), 0, 3)
    counts = jnp.minimum(lowest[:, None] + extra, MAXB)
    counts = counts.at[0, forced_column(key)].set(MAXB)
    return counts.astype(jnp.int32)


def draw_blk_offset(key, part):
    distance = band_distance()
    denom = max((N_LAT - 1) ** 2, 1)
    reach = 1 + (RMAX - 1) * distance * distance // denom
    raw = jax.random.randint(jax.random.fold_in(key, 2), (N_LAT, N_LON, MAXB), 0, 2 * RMAX + 1)
    offsets = raw % (2 * reach[:, None, None] + 1) - reach[:, None, None]
    column = forced_column(key)
    offsets = offsets.at[0, column, 0].set(RMAX)
    offsets = offsets.at[0, column, 1].set(-RMAX)
    return offsets.astype(jnp.int32)


def draw_hidden_init(key, part):
    shape = (NLAT, NLON, H)
    values = jax.random.uniform(jax.random.fold_in(key, 11), shape, jnp.float32, -1.0, 1.0)
    return values.astype(jnp.bfloat16)


def place_ends(drawn, own_key, smallest, top_value):
    shape = drawn.shape
    spot = [jax.random.randint(jax.random.fold_in(own_key, axis), (), 0, shape[axis]) for axis in range(len(shape))]
    drawn = drawn.at[tuple(spot)].set(smallest)
    longest = shape.index(max(shape))
    spot[longest] = (spot[longest] + 1) % shape[longest]
    return drawn.at[tuple(spot)].set(top_value)


def levels(rng, extent, split, low, high):
    level = 1.0
    for position, parts in split:
        heights = jax.random.uniform(jax.random.fold_in(jax.random.fold_in(rng, 6), position), (parts,), jnp.float32, low / len(split), high / len(split))
        level = level * jnp.repeat(jnp.exp(heights), extent[position] // parts).reshape((-1,) + (1,) * (len(extent) - 1 - position))
    return level


def bell_draw(key, extent, scale, most, split=(), kind=jnp.bfloat16):
    loudness = levels(key, extent, split, -0.22, 0.18) if split else 1.0
    result = jax.random.normal(key, extent, jnp.float32) * scale * loudness
    return jnp.minimum(jnp.maximum(result, -most), most).astype(kind)


def setup_inputs(seed: int = 0) -> dict:
    seeds = jax.random.split(jax.random.key(seed), 14)
    return {
        "feat_one": bell_draw(seeds[0], (NLAT, NLON, C), 1.0, 6.0, ((0, 4), (1, 8))),
        "feat_two": bell_draw(seeds[1], (NLAT, NLON, C), 1.0, 6.0, ((0, 4), (1, 8))),
        "context_in": jnp.clip(2.0 * jax.random.uniform(seeds[2], (NLAT, NLON, H), jnp.float32) ** levels(seeds[2], (NLAT, NLON, H), ((0, 4), (1, 8)), -0.2, 0.2), 0.0, 2.0).astype(jnp.bfloat16),
        "hidden_init": draw_hidden_init(jax.random.fold_in(seeds[13], 71), 0),
        "corr_proj": bell_draw(seeds[4], (NCLASS, POOLR * POOLC, H), (POOLR * POOLC) ** -0.5, 0.5),
        "input_conv": bell_draw(seeds[5], (2, 5, 2 * H, 3 * H), (15 * H) ** -0.5, 0.125),
        "state_zr": bell_draw(seeds[6], (2, 5, H, 2 * H), (H // 2) ** -0.5, 0.75),
        "state_q": bell_draw(seeds[7], (2, 5, H, H), (H // 2) ** -0.5, 0.75),
        "update_bias": jnp.clip(jax.random.uniform(seeds[8], (2, H), jnp.float32, -2.0, 0.0), -2.0, 0.0),
        "gate_bias": bell_draw(seeds[9], (2, 2 * H), 0.5, 3.0, (), jnp.float32),
        "blk_offset": draw_blk_offset(jax.random.fold_in(seeds[13], 71), 0),
        "blk_class": place_ends(jax.random.randint(seeds[11], (N_LAT, N_LON, MAXB), 0, NCLASS), jax.random.fold_in(seeds[11], 1), 0, NCLASS - 1).astype(jnp.int32),
        "blk_count": draw_blk_count(jax.random.fold_in(seeds[13], 71), 0),
    }


def conv_lon(values, weight):
    width = values.shape[1]
    padded = jnp.concatenate([values[:, width - 2:], values, values[:, :2]], axis=1)
    total = jnp.zeros((values.shape[0] * width, weight.shape[2]), jnp.float32)
    for tap in range(5):
        piece = padded[:, tap:tap + width].reshape(-1, values.shape[2])
        total = total + jnp.dot(piece, weight[tap], preferred_element_type=jnp.float32)
    return total


def conv_lat(values, weight):
    height = values.shape[0]
    padded = jnp.pad(values, ((2, 2), (0, 0), (0, 0)))
    total = jnp.zeros((height * values.shape[1], weight.shape[2]), jnp.float32)
    for tap in range(5):
        piece = padded[tap:tap + height].reshape(-1, values.shape[2])
        total = total + jnp.dot(piece, weight[tap], preferred_element_type=jnp.float32)
    return total


def gru_pass(state, inputs, conv, zr_weight, q_weight, z_bias, gate_row, shape):
    hid = state.shape[1]
    state_bf = state.astype(jnp.bfloat16).reshape(shape)
    mixed = conv(state_bf, zr_weight)
    update = jax.nn.sigmoid(inputs[:, :hid] + mixed[:, :hid] + z_bias)
    reset = jax.nn.sigmoid(inputs[:, hid:2 * hid] + mixed[:, hid:] + gate_row[:hid])
    reset_state = (reset * state).astype(jnp.bfloat16).reshape(shape)
    candidate = jnp.tanh(inputs[:, 2 * hid:] + conv(reset_state, q_weight) + gate_row[hid:])
    return (1.0 - update) * state + update * candidate


def reference(feat_one, feat_two, context_in, hidden_init, corr_proj, input_conv, state_zr, state_q, update_bias, gate_bias, blk_offset, blk_class, blk_count):
    pool_rows = ROWS // POOLR
    pool_cols = COLS // POOLC
    points = POOLR * POOLC

    def band_motion(inputs):
        first, second, offsets, classes, counts = inputs
        queries = first.reshape(ROWS, N_LON, COLS, C).transpose(1, 0, 2, 3).reshape(N_LON, ROWS * COLS, C).astype(jnp.float32)
        grid = second.reshape(POOLR, pool_rows, N_LON, POOLC, pool_cols, C)
        pooled = (jnp.sum(grid, axis=(1, 4), dtype=jnp.float32) / (pool_rows * pool_cols)).astype(jnp.bfloat16)
        pooled = pooled.transpose(1, 0, 2, 3).reshape(N_LON, points, C)
        panels = jnp.arange(N_LON, dtype=jnp.int32)
        total = jnp.zeros((N_LON, ROWS * COLS, H), jnp.float32)
        for slot in range(MAXB):
            target = ((panels + offsets[:, slot]) % N_LON).astype(jnp.int32)
            keys = jnp.take(pooled, target, axis=0).astype(jnp.float32)
            corr = (jnp.einsum("nqc,npc->nqp", queries, keys) * (C ** -0.5)).astype(jnp.bfloat16)
            proj = jnp.take(corr_proj, classes[:, slot], axis=0).astype(jnp.float32)
            term = jnp.einsum("nqp,nph->nqh", corr.astype(jnp.float32), proj)
            total = total + jnp.where((slot < counts)[:, None, None], term, jnp.float32(0.0))
        motion = jnp.maximum(total, 0.0).astype(jnp.bfloat16)
        return motion.reshape(N_LON, ROWS, COLS, H).transpose(1, 0, 2, 3).reshape(ROWS, N_LON * COLS, H)

    motion = lax.map(band_motion, (feat_one.reshape(N_LAT, ROWS, NLON, C), feat_two.reshape(N_LAT, ROWS, NLON, C), blk_offset, blk_class, blk_count))
    motion = motion.reshape(NLAT, NLON, H)
    joined = jnp.concatenate([context_in, motion], axis=2)
    x_lon = conv_lon(joined, input_conv[0])
    x_lat = conv_lat(joined, input_conv[1])
    shape = (NLAT, NLON, H)
    state = hidden_init.astype(jnp.float32).reshape(-1, H)
    for step in range(ITERS):
        state = gru_pass(state, x_lon, conv_lon, state_zr[0], state_q[0], update_bias[0], gate_bias[0], shape)
        state = gru_pass(state, x_lat, conv_lat, state_zr[1], state_q[1], update_bias[1], gate_bias[1], shape)
    return state.astype(jnp.bfloat16).reshape(shape)
```

```python
import functools

import jax
import jax.numpy as jnp
from jax import lax
from jax.experimental import pallas as pl
from jax.experimental.pallas import tpu as pltpu
from jax.sharding import PartitionSpec as P

POOLR = 8
POOLC = 16
RMAX = 4
ITERS = 4
HALO = 4
EDGE = 16
CTX, HID, MOT, STATE = 0, 1, 2, 3
MESH = pl.DeviceIdType.MESH
BF = jnp.bfloat16
F32 = jnp.float32


def sigmoid(value):
    return 0.5 * jnp.tanh(0.5 * value) + 0.5


def dot(left, right):
    return jnp.dot(left, right, preferred_element_type=F32)


def flat(value):
    return value.reshape(-1, value.shape[-1])


def kernel(
    n_lat,
    n_lon,
    offset_ref,
    class_ref,
    count_ref,
    one_ref,
    two_ref,
    ctx_ref,
    init_ref,
    proj_ref,
    input_ref,
    zr_ref,
    q_ref,
    ubias_ref,
    gbias_ref,
    out_ref,
    ext,
    side_l,
    side_r,
    pool,
    corr,
    projs,
    joined,
    xl_z,
    xl_r,
    xl_q,
    xt_z,
    xt_r,
    xt_q,
    s_lon,
    s_lat,
    rs_lon,
    rs_lat,
    z_lon,
    z_lat,
    send_sem,
    recv_sem,
    pool_send,
    pool_recv,
    pass_send,
):
    rows, cols, chans = one_ref.shape
    hid = init_ref.shape[2]
    wide = cols + 16
    near = cols + 8
    slots = offset_ref.shape[2]
    lat, lon = lax.axis_index("lat"), lax.axis_index("lon")
    north, south = lax.rem(lat + n_lat - 1, n_lat), lax.rem(lat + 1, n_lat)
    west, east = lax.rem(lon + n_lon - 1, n_lon), lax.rem(lon + 1, n_lon)
    has_n, has_s = lat > 0, lat < n_lat - 1
    parity = lax.rem(lon, 2)
    lowest = -min(RMAX, (n_lon - 1) // 2)
    highest = min(RMAX, n_lon // 2)

    def place(offset):
        return lax.rem(offset - lowest + n_lon, n_lon)

    def along(steps):
        return lax.rem(lon + steps + n_lon, n_lon)

    evens = [d for d in (2, -2, 4, -4) if lowest <= d <= highest]

    barrier = pltpu.get_barrier_semaphore()
    partners = [1, -1] + evens
    for steps in partners:
        pl.semaphore_signal(
            barrier, inc=1, device_id=(lat, along(steps)), device_id_type=MESH
        )

    @pl.when(has_n)
    def _():
        for column in (west, lon, east):
            pl.semaphore_signal(barrier, inc=1, device_id=(north, column), device_id_type=MESH)

    @pl.when(has_s)
    def _():
        for column in (west, lon, east):
            pl.semaphore_signal(barrier, inc=1, device_id=(south, column), device_id_type=MESH)

    top = slice(HALO, 2 * HALO)
    bottom = slice(rows, rows + HALO)
    above = slice(0, HALO)
    below = slice(rows + HALO, rows + 2 * HALO)
    body = slice(HALO, HALO + rows)
    first, last = slice(0, EDGE), slice(cols - EDGE, cols)
    panel = slice(0, cols)

    def copy(e, way):
        src, dst, device = (
            lambda: (ext.at[e, top, panel], ext.at[e, below, panel], (north, lon)),
            lambda: (ext.at[e, bottom, panel], ext.at[e, above, panel], (south, lon)),
            lambda: (ext.at[e, body, last], side_l.at[e, body], (lat, east)),
            lambda: (ext.at[e, body, first], side_r.at[e, body], (lat, west)),
            lambda: (ext.at[e, top, last], side_l.at[e, below], (north, east)),
            lambda: (ext.at[e, top, first], side_r.at[e, below], (north, west)),
            lambda: (ext.at[e, bottom, last], side_l.at[e, above], (south, east)),
            lambda: (ext.at[e, bottom, first], side_r.at[e, above], (south, west)),
        )[way]()
        return pltpu.make_async_remote_copy(
            src_ref=src,
            dst_ref=dst,
            send_sem=send_sem.at[e, way],
            recv_sem=recv_sem.at[e, way],
            device_id=device,
            device_id_type=MESH,
        )

    to_north, to_south, to_side = (0, 4, 5), (1, 6, 7), (2, 3)

    def send(e, full=True):
        if full:

            @pl.when(has_n)
            def _():
                for way in to_north:
                    copy(e, way).start()

            @pl.when(has_s)
            def _():
                for way in to_south:
                    copy(e, way).start()

        for way in to_side:
            copy(e, way).start()

    def receive(e, full=True):
        if full:

            @pl.when(has_s)
            def _():
                for way in to_north:
                    copy(e, way).wait_recv()
                for way in to_south:
                    copy(e, way).wait_send()

            @pl.when(jnp.logical_not(has_s))
            def _():
                ext[e, below] = jnp.zeros((HALO, wide, hid), BF)
                side_l[e, below] = jnp.zeros((HALO, EDGE, hid), BF)
                side_r[e, below] = jnp.zeros((HALO, EDGE, hid), BF)

            @pl.when(has_n)
            def _():
                for way in to_south:
                    copy(e, way).wait_recv()
                for way in to_north:
                    copy(e, way).wait_send()

            @pl.when(jnp.logical_not(has_n))
            def _():
                ext[e, above] = jnp.zeros((HALO, wide, hid), BF)
                side_l[e, above] = jnp.zeros((HALO, EDGE, hid), BF)
                side_r[e, above] = jnp.zeros((HALO, EDGE, hid), BF)

        for way in to_side:
            copy(e, way).wait()
        part = slice(None) if full else body
        right = side_r[e, part].astype(F32)
        left = side_l[e, part].astype(F32)
        spot = lax.broadcasted_iota(jnp.int32, right.shape, 1)
        merged = jnp.where(spot < 8, right, left)
        ext[e, part, cols:] = merged.astype(BF)

    def spread(e, target):
        target[:, 8 : 8 + cols] = ext[e, body, panel].astype(F32)
        sides = ext[e, body, cols:].astype(F32)
        target[:, 8 + cols :] = sides[:, 0:8]
        target[:, 0:8] = sides[:, 8:16]

    point = lax.broadcasted_iota(jnp.int32, (POOLC, 2 * cols), 0)
    cell = lax.rem(lax.broadcasted_iota(jnp.int32, (POOLC, 2 * cols), 1), cols)
    pool_rows, pool_cols = rows // POOLR, cols // POOLC
    inside = (cell >= point * pool_cols) & (cell < (point + 1) * pool_cols)
    window = jnp.where(inside, 1.0 / (pool_rows * pool_cols), 0.0).astype(BF)
    for index in range(POOLR):
        block = flat(two_ref[pool_rows * index : pool_rows * (index + 1)])
        pool[-lowest, POOLC * index : POOLC * (index + 1)] = dot(window, block).astype(BF)
    ext[CTX, body, panel] = ctx_ref[...]
    ext[HID, body, panel] = init_ref[...]

    lat_partners = 3 * has_n.astype(jnp.int32) + 3 * has_s.astype(jnp.int32)
    pl.semaphore_wait(barrier, len(partners) + lat_partners)

    def direct(steps):
        return pltpu.make_async_remote_copy(
            src_ref=pool.at[-lowest],
            dst_ref=pool.at[place(-steps)],
            send_sem=pool_send.at[evens.index(steps)],
            recv_sem=pool_recv.at[place(-steps)],
            device_id=(lat, along(steps)),
            device_id_type=MESH,
        )

    sibling = lon + 1 - 2 * parity

    def forward(number, source):
        target = source - 1 + 2 * parity
        return pltpu.make_async_remote_copy(
            src_ref=pool.at[place(source)],
            dst_ref=pool.at[place(target)],
            send_sem=pass_send.at[number],
            recv_sem=pool_recv.at[place(target)],
            device_id=(lat, sibling),
            device_id_type=MESH,
        )

    def arrived(spot):
        return pltpu.make_async_remote_copy(
            src_ref=pool.at[-lowest],
            dst_ref=pool.at[spot],
            send_sem=pool_send.at[0],
            recv_sem=pool_recv.at[spot],
            device_id=(lat, sibling),
            device_id_type=MESH,
        ).wait_recv()

    send(CTX)
    for steps in evens:
        direct(steps).start()
    forward(0, 0).start()
    send(HID, False)

    def inputs_lon(part, base):
        weight = [
            input_ref[0, tap, part * hid : (part + 1) * hid, :] for tap in range(5)
        ]
        weight = jnp.concatenate(weight, axis=0)
        step = rows // 2

        def chunk(index, carry):
            at = pl.ds(index * step, step)
            pieces = [flat(joined[at, 2 + k : 2 + k + near]).astype(BF) for k in range(5)]
            total = dot(jnp.concatenate(pieces, axis=1), weight)
            for place_, store in enumerate((xl_z, xl_r, xl_q)):
                value = total[:, place_ * hid : (place_ + 1) * hid].reshape(step, near, hid)
                if base is None:
                    store[at] = store[at] + value
                else:
                    store[at] = value + base[place_]
            return carry

        lax.fori_loop(0, 2, chunk, 0)

    def inputs_lat(part, e, base):
        weight = [
            input_ref[1, tap, part * hid : (part + 1) * hid, :] for tap in range(5)
        ]
        weight = jnp.concatenate(weight, axis=0)
        step = (rows + 4) // 2

        def chunk(index, carry):
            start = index * step
            at = pl.ds(start, step)
            pieces = [flat(ext[e, pl.ds(start + k, step)]) for k in range(5)]
            total = dot(jnp.concatenate(pieces, axis=1), weight)
            for place_, store in enumerate((xt_z, xt_r, xt_q)):
                value = total[:, place_ * hid : (place_ + 1) * hid].reshape(step, wide, hid)
                if base is None:
                    store[at] = store[at] + value
                else:
                    store[at] = value + base[place_]
            return carry

        lax.fori_loop(0, 2, chunk, 0)

    def biases(index):
        gate = gbias_ref[index : index + 1]
        parts = ubias_ref[index : index + 1], gate[:, :hid], gate[:, hid:]
        return [part.reshape(1, 1, hid) for part in parts]

    receive(CTX)
    spread(CTX, joined)
    inputs_lon(0, biases(0))
    inputs_lat(0, CTX, biases(1))

    scale = chans ** (-0.5)

    def correlate(spot):
        keys = pool[spot]
        step = rows // 4

        def chunk(index, carry):
            queries = flat(one_ref[pl.ds(index * step, step)])
            value = lax.dot_general(
                queries, keys, (((1,), (1,)), ((), ())), preferred_element_type=F32
            )
            corr[spot, pl.ds(index * step, step)] = (
                (value * scale).astype(BF).reshape(step, cols, -1)
            )
            return carry

        lax.fori_loop(0, 4, chunk, 0)

    correlate(-lowest)
    sources = [-2, 2, 4 - 8 * parity]
    for number, source in enumerate(sources):
        arrived(place(source))
        forward(number + 1, source).start()
    if n_lon > 2 * RMAX:
        arrived(place(4 * (2 * parity - 1)))
    for steps in evens:
        correlate(place(steps))
    for steps in (-1, 1, -3, 3):
        arrived(place(steps))
        correlate(place(steps))
    for steps in evens:
        direct(steps).wait_send()
    for number, source in enumerate([0] + sources):
        forward(number, source).wait_send()

    live = count_ref[0, 0]
    spots = []
    for slot in range(slots):
        offset = offset_ref[0, 0, slot]
        spots.append(jnp.where(offset < lowest, offset + n_lon, offset) - lowest)
        weight = proj_ref[class_ref[0, 0, slot]].astype(F32)
        weight = jnp.where(slot < live, weight, 0.0)
        projs[slot * weight.shape[0] : (slot + 1) * weight.shape[0]] = weight.astype(BF)

    quarter = rows // 4

    def move(index, carry):
        at = pl.ds(index * quarter, quarter)
        pieces = [flat(corr[spot, at]) for spot in spots]
        total = dot(jnp.concatenate(pieces, axis=1), projs[...])
        moved = jnp.maximum(total, 0.0).astype(BF).reshape(quarter, cols, hid)
        ext[MOT, pl.ds(HALO + index * quarter, quarter), panel] = moved
        return carry

    lax.fori_loop(0, 4, move, 0)
    send(MOT)
    receive(HID, False)
    spread(HID, s_lon)
    receive(MOT)
    spread(MOT, joined)
    inputs_lon(1, None)
    inputs_lat(1, MOT, None)

    def pass_lon(e):
        step = rows // 2

        def gates(index, carry):
            at = pl.ds(index * step, step)
            pieces = [flat(s_lon[at, 2 + k : 2 + k + near]).astype(BF) for k in range(5)]
            mixed = dot(jnp.concatenate(pieces, axis=1), zr_ref[0])
            z_lon[at] = sigmoid(xl_z[at] + mixed[:, :hid].reshape(step, near, hid))
            reset = sigmoid(xl_r[at] + mixed[:, hid:].reshape(step, near, hid))
            rs_lon[at] = reset * s_lon[at, 4 : 4 + near]
            return carry

        lax.fori_loop(0, 2, gates, 0)

        def update(index, carry):
            at = pl.ds(index * step, step)
            pieces = [flat(rs_lon[at, 2 + k : 2 + k + cols]).astype(BF) for k in range(5)]
            mixed = dot(jnp.concatenate(pieces, axis=1), q_ref[0]).reshape(step, cols, hid)
            candidate = jnp.tanh(xl_q[at, 4 : 4 + cols] + mixed)
            state = s_lon[at, 8 : 8 + cols]
            z = z_lon[at, 4 : 4 + cols]
            state = (1.0 - z) * state + z * candidate
            inner = pl.ds(HALO + index * step, step)
            s_lat[inner, panel] = state
            ext[e, inner, panel] = state.astype(BF)
            return carry

        lax.fori_loop(0, 2, update, 0)

    def pass_lat(e):
        s_lat[above] = ext[e, above].astype(F32)
        s_lat[below] = ext[e, below].astype(F32)
        s_lat[body, cols:] = ext[e, body, cols:].astype(F32)
        step = (rows + 4) // 2

        def gates(index, carry):
            start = index * step
            at = pl.ds(start, step)
            pieces = [flat(ext[e, pl.ds(start + k, step)]) for k in range(5)]
            mixed = dot(jnp.concatenate(pieces, axis=1), zr_ref[1])
            z_lat[at] = sigmoid(xt_z[at] + mixed[:, :hid].reshape(step, wide, hid))
            reset = sigmoid(xt_r[at] + mixed[:, hid:].reshape(step, wide, hid))
            rs_lat[at] = (reset * s_lat[pl.ds(start + 2, step)]).astype(BF)
            return carry

        lax.fori_loop(0, 2, gates, 0)
        half = rows // 2

        def update(index, carry):
            start = index * half
            at = pl.ds(start, half)
            pieces = [flat(rs_lat[pl.ds(start + k, half)]) for k in range(5)]
            mixed = dot(jnp.concatenate(pieces, axis=1), q_ref[1]).reshape(half, wide, hid)
            candidate = jnp.tanh(xt_q[pl.ds(start + 2, half)] + mixed)
            state = s_lat[pl.ds(start + HALO, half)]
            z = z_lat[pl.ds(start + 2, half)]
            state = (1.0 - z) * state + z * candidate
            s_lon[at, 8 : 8 + cols] = state[:, panel]
            s_lon[at, 8 + cols :] = state[:, cols : cols + 8]
            s_lon[at, 0:8] = state[:, cols + 8 :]
            return carry

        lax.fori_loop(0, 2, update, 0)

    def iteration(index, carry):
        e = STATE + index
        pass_lon(e)
        send(e)
        receive(e)
        pass_lat(e)
        return carry

    lax.fori_loop(0, ITERS, iteration, 0)
    out_ref[...] = s_lon[:, 8 : 8 + cols].astype(BF)


def local(
    n_lat,
    n_lon,
    feat_one,
    feat_two,
    context_in,
    hidden_init,
    corr_proj,
    input_conv,
    state_zr,
    state_q,
    update_bias,
    gate_bias,
    blk_offset,
    blk_class,
    blk_count,
):
    rows, cols, chans = feat_one.shape
    hid = hidden_init.shape[2]
    points = POOLR * POOLC
    slots = blk_offset.shape[2]
    reach = min(n_lon, 2 * RMAX + 1)
    wide, near = cols + 16, cols + 8
    tall = rows + 2 * HALO
    count = STATE + ITERS
    taps = state_zr.shape[1]
    state_zr = state_zr.reshape(2, taps * hid, 2 * hid)
    state_q = state_q.reshape(2, taps * hid, hid)
    vmem = pl.BlockSpec(memory_space=pltpu.VMEM)
    smem = pl.BlockSpec(memory_space=pltpu.SMEM)
    return pl.pallas_call(
        functools.partial(kernel, n_lat, n_lon),
        out_shape=jax.ShapeDtypeStruct((rows, cols, hid), BF),
        in_specs=[smem] * 3 + [vmem] * 10,
        out_specs=vmem,
        scratch_shapes=[
            pltpu.VMEM((count, tall, wide, hid), BF),
            pltpu.VMEM((count, tall, EDGE, hid), BF),
            pltpu.VMEM((count, tall, EDGE, hid), BF),
            pltpu.VMEM((reach, points, chans), BF),
            pltpu.VMEM((reach, rows, cols, points), BF),
            pltpu.VMEM((slots * points, hid), BF),
            pltpu.VMEM((rows, wide, hid), F32),
            pltpu.VMEM((rows, near, hid), F32),
            pltpu.VMEM((rows, near, hid), F32),
            pltpu.VMEM((rows, near, hid), F32),
            pltpu.VMEM((rows + 4, wide, hid), F32),
            pltpu.VMEM((rows + 4, wide, hid), F32),
            pltpu.VMEM((rows + 4, wide, hid), F32),
            pltpu.VMEM((rows, wide, hid), F32),
            pltpu.VMEM((tall, wide, hid), F32),
            pltpu.VMEM((rows, near, hid), F32),
            pltpu.VMEM((rows + 4, wide, hid), BF),
            pltpu.VMEM((rows, near, hid), F32),
            pltpu.VMEM((rows + 4, wide, hid), F32),
            pltpu.SemaphoreType.DMA((count, 8)),
            pltpu.SemaphoreType.DMA((count, 8)),
            pltpu.SemaphoreType.DMA((4,)),
            pltpu.SemaphoreType.DMA((reach,)),
            pltpu.SemaphoreType.DMA((4,)),
        ],
        compiler_params=pltpu.CompilerParams(
            collective_id=0, has_side_effects=True, vmem_limit_bytes=52 * 1024 * 1024
        ),
        name="refine",
    )(
        blk_offset,
        blk_class,
        blk_count,
        feat_one,
        feat_two,
        context_in,
        hidden_init,
        corr_proj,
        input_conv,
        state_zr,
        state_q,
        update_bias,
        gate_bias,
    )


def solution(mesh):
    placed = (
        P("lat", "lon", None),
        P("lat", "lon", None),
        P("lat", "lon", None),
        P("lat", "lon", None),
        P(),
        P(),
        P(),
        P(),
        P(),
        P(),
        P("lat", "lon", None),
        P("lat", "lon", None),
        P("lat", "lon"),
    )
    return jax.shard_map(
        functools.partial(local, mesh.shape["lat"], mesh.shape["lon"]),
        mesh=mesh,
        in_specs=placed,
        out_specs=P("lat", "lon", None),
        check_vma=False,
    )
```

```python
import functools

import jax
import jax.numpy as jnp
from jax import lax
from jax.experimental import pallas as pl
from jax.experimental.pallas import tpu as pltpu
from jax.sharding import PartitionSpec as P

POOLR = 8
POOLC = 16
RMAX = 4
ITERS = 4
HALO = 4
CTX, MOT, STATE = 0, 1, 2
MESH = pl.DeviceIdType.MESH
BF = jnp.bfloat16
F32 = jnp.float32


def sigmoid(value):
    return 0.5 * jnp.tanh(0.5 * value) + 0.5


def dot(left, right):
    return jnp.dot(left, right, preferred_element_type=F32)


def flat(value):
    return value.reshape(-1, value.shape[-1])


def joined_up(parts, axis):
    return parts[0] if len(parts) == 1 else jnp.concatenate(parts, axis=axis)


def kernel(
    n_lat,
    n_lon,
    offset_ref,
    class_ref,
    count_ref,
    one_hbm,
    two_hbm,
    ctx_hbm,
    init_hbm,
    proj_hbm,
    input_hbm,
    zr_hbm,
    q_hbm,
    ubias_ref,
    gbias_ref,
    out_ref,
    one_ref,
    two_ref,
    init_ref,
    proj_ref,
    input_ref,
    zr_ref,
    q_ref,
    ext,
    side_out,
    side_in,
    pool,
    corr,
    projs,
    joined,
    xl_z,
    xl_r,
    xl_q,
    xt_z,
    xt_r,
    xt_q,
    s_lon,
    s_lat,
    rs_lon,
    rs_lat,
    z_lon,
    z_lat,
    load_sem,
    ns_send,
    ns_recv,
    ew_send,
    ew_recv,
    pool_send,
    pool_recv,
    pass_send,
):
    rows, cols, chans = one_ref.shape
    hid = init_ref.shape[2]
    near = cols + 8
    slots = offset_ref.shape[2]
    lat, lon = lax.axis_index("lat"), lax.axis_index("lon")
    north, south = lax.rem(lat + n_lat - 1, n_lat), lax.rem(lat + 1, n_lat)
    west, east = lax.rem(lon + n_lon - 1, n_lon), lax.rem(lon + 1, n_lon)
    has_n, has_s = lat > 0, lat < n_lat - 1
    parity = lax.rem(lon, 2)
    lowest = -min(RMAX, (n_lon - 1) // 2)
    highest = min(RMAX, n_lon // 2)

    top = slice(HALO, 2 * HALO)
    bottom = slice(rows, rows + HALO)
    above = slice(0, HALO)
    below = slice(rows + HALO, rows + 2 * HALO)
    body = slice(HALO, HALO + rows)
    main = slice(8, 8 + cols)

    loads = [
        pltpu.make_async_copy(source, target, load_sem.at[number])
        for number, (source, target) in enumerate(
            (
                (two_hbm, two_ref),
                (ctx_hbm, ext.at[CTX, body]),
                (init_hbm, init_ref),
                (input_hbm, input_ref),
                (one_hbm, one_ref),
                (proj_hbm, proj_ref),
                (zr_hbm, zr_ref),
                (q_hbm, q_ref),
            )
        )
    ]
    for load in loads:
        load.start()

    def place(offset):
        return lax.rem(offset - lowest + n_lon, n_lon)

    def along(steps):
        return lax.rem(lon + steps + n_lon, n_lon)

    evens = [d for d in (2, -2, 4, -4) if lowest <= d <= highest]

    barrier = pltpu.get_barrier_semaphore()
    partners = [1, -1] + evens
    for steps in partners:
        pl.semaphore_signal(
            barrier, inc=1, device_id=(lat, along(steps)), device_id_type=MESH
        )

    @pl.when(has_n)
    def _():
        pl.semaphore_signal(barrier, inc=1, device_id=(north, lon), device_id_type=MESH)

    @pl.when(has_s)
    def _():
        pl.semaphore_signal(barrier, inc=1, device_id=(south, lon), device_id_type=MESH)

    def to_lat(e, way):
        return pltpu.make_async_remote_copy(
            src_ref=ext.at[e, bottom if way else top],
            dst_ref=ext.at[e, above if way else below],
            send_sem=ns_send.at[e, way],
            recv_sem=ns_recv.at[e, way],
            device_id=(south if way else north, lon),
            device_id_type=MESH,
        )

    def to_lon(e, way):
        return pltpu.make_async_remote_copy(
            src_ref=side_out.at[e, way],
            dst_ref=side_in.at[e, 1 - way],
            send_sem=ew_send.at[e, way],
            recv_sem=ew_recv.at[e, way],
            device_id=(lat, east if way else west),
            device_id_type=MESH,
        )

    def send_lat(e):
        @pl.when(has_n)
        def _():
            to_lat(e, 0).start()

        @pl.when(has_s)
        def _():
            to_lat(e, 1).start()

    def receive_lat(e):
        @pl.when(has_s)
        def _():
            to_lat(e, 0).wait_recv()
            to_lat(e, 1).wait_send()

        @pl.when(jnp.logical_not(has_s))
        def _():
            ext[e, below] = jnp.zeros((HALO, cols, hid), BF)

        @pl.when(has_n)
        def _():
            to_lat(e, 1).wait_recv()
            to_lat(e, 0).wait_send()

        @pl.when(jnp.logical_not(has_n))
        def _():
            ext[e, above] = jnp.zeros((HALO, cols, hid), BF)

    def send_lon(e, low, high):
        for way, value in enumerate((low, high)):
            side_out[e, way] = value.reshape(rows // 2, 16, hid).astype(BF)
        for way in range(2):
            to_lon(e, way).start()

    def receive_lon(e, target):
        for way in range(2):
            to_lon(e, way).wait()
        target[:, 0:8] = side_in[e, 0].astype(F32).reshape(rows, 8, hid)
        target[:, 8 + cols :] = side_in[e, 1].astype(F32).reshape(rows, 8, hid)

    def direct(steps):
        return pltpu.make_async_remote_copy(
            src_ref=pool.at[-lowest],
            dst_ref=pool.at[place(-steps)],
            send_sem=pool_send.at[evens.index(steps)],
            recv_sem=pool_recv.at[place(-steps)],
            device_id=(lat, along(steps)),
            device_id_type=MESH,
        )

    sibling = lon + 1 - 2 * parity

    def forward(number, source):
        target = source - 1 + 2 * parity
        return pltpu.make_async_remote_copy(
            src_ref=pool.at[place(source)],
            dst_ref=pool.at[place(target)],
            send_sem=pass_send.at[number],
            recv_sem=pool_recv.at[place(target)],
            device_id=(lat, sibling),
            device_id_type=MESH,
        )

    def arrived(spot):
        return pltpu.make_async_remote_copy(
            src_ref=pool.at[-lowest],
            dst_ref=pool.at[spot],
            send_sem=pool_send.at[0],
            recv_sem=pool_recv.at[spot],
            device_id=(lat, sibling),
            device_id_type=MESH,
        ).wait_recv()

    point = lax.broadcasted_iota(jnp.int32, (POOLC, 2 * cols), 0)
    cell = lax.rem(lax.broadcasted_iota(jnp.int32, (POOLC, 2 * cols), 1), cols)
    pool_rows, pool_cols = rows // POOLR, cols // POOLC
    inside = (cell >= point * pool_cols) & (cell < (point + 1) * pool_cols)
    window = jnp.where(inside, 1.0 / (pool_rows * pool_cols), 0.0).astype(BF)
    loads[0].wait()
    for index in range(POOLR):
        block = flat(two_ref[pool_rows * index : pool_rows * (index + 1)])
        pool[-lowest, POOLC * index : POOLC * (index + 1)] = dot(window, block).astype(BF)

    lat_partners = has_n.astype(jnp.int32) + has_s.astype(jnp.int32)
    pl.semaphore_wait(barrier, len(partners) + lat_partners)
    for steps in evens:
        direct(steps).start()
    forward(0, 0).start()
    loads[1].wait()
    send_lat(CTX)
    whole = ext[CTX, body].astype(F32)
    joined[:, main] = whole
    send_lon(CTX, whole[:, 0:8], whole[:, cols - 8 :])
    loads[2].wait()
    whole = init_ref[...].astype(F32)
    s_lon[:, main] = whole
    send_lon(STATE, whole[:, 0:8], whole[:, cols - 8 :])

    def weights(index, part):
        channels = slice(part * hid, (part + 1) * hid)
        return jnp.concatenate([input_ref[index, tap, channels, :] for tap in range(5)], axis=0)

    def biases(index):
        gate = gbias_ref[index : index + 1]
        parts = ubias_ref[index : index + 1], gate[:, :hid], gate[:, hid:]
        return [part.reshape(1, 1, hid) for part in parts]

    def keep(stores, at, total, shape, base):
        for number, store in enumerate(stores):
            value = total[:, number * hid : (number + 1) * hid].reshape(shape)
            store[at] = value + (store[at] if base is None else base[number])

    def inputs_lon(part, base):
        weight = weights(0, part)
        step = rows // 2

        def chunk(index, carry):
            at = pl.ds(index * step, step)
            pieces = [flat(joined[at, 2 + k : 2 + k + near]).astype(BF) for k in range(5)]
            total = dot(jnp.concatenate(pieces, axis=1), weight)
            keep((xl_z, xl_r, xl_q), at, total, (step, near, hid), base)
            return carry

        lax.fori_loop(0, 2, chunk, 0)

    def inputs_lat(part, e, base, blocks):
        weight = weights(1, part)
        for start, size in blocks:
            pieces = [flat(ext[e, start + k : start + k + size]) for k in range(5)]
            total = dot(jnp.concatenate(pieces, axis=1), weight)
            at = slice(start, start + size)
            keep((xt_z, xt_r, xt_q), at, total, (size, cols, hid), base)

    inner = ((4, rows // 2 - 2), (rows // 2 + 2, rows // 2 - 2))
    outer = ((0, 4), (rows, 4))

    loads[3].wait()
    inputs_lat(0, CTX, biases(1), inner)
    sources = [-2, 2, 4 - 8 * parity]

    def hand_on(number):
        arrived(place(sources[number]))
        forward(number + 1, sources[number]).start()

    receive_lon(CTX, joined)
    hand_on(0)
    hand_on(1)
    inputs_lon(0, biases(0))
    hand_on(2)
    receive_lat(CTX)
    inputs_lat(0, CTX, biases(1), outer)

    scale = chans ** (-0.5)

    def correlate(*spots):
        keys = joined_up([pool[spot] for spot in spots], 0)
        points = pool.shape[1]
        step = rows // 4

        def chunk(index, carry):
            at = pl.ds(index * step, step)
            value = lax.dot_general(
                flat(one_ref[at]), keys, (((1,), (1,)), ((), ())), preferred_element_type=F32
            )
            value = (value * scale).astype(BF)
            for number, spot in enumerate(spots):
                part = value[:, number * points : (number + 1) * points]
                corr[spot, at] = part.reshape(step, cols, points)
            return carry

        lax.fori_loop(0, 4, chunk, 0)

    loads[4].wait()
    correlate(place(0), place(2))
    if n_lon > 2 * RMAX:
        arrived(place(4 * (2 * parity - 1)))
        correlate(place(-4))
    correlate(place(-2), place(4))
    for pair in ((-1, 1), (-3, 3)):
        for steps in pair:
            arrived(place(steps))
        correlate(*[place(steps) for steps in pair])

    loads[5].wait()
    live = count_ref[0, 0]
    spots = []
    for slot in range(slots):
        offset = offset_ref[0, 0, slot]
        spots.append(jnp.where(offset < lowest, offset + n_lon, offset) - lowest)
        weight = proj_ref[class_ref[0, 0, slot]].astype(F32)
        weight = jnp.where(slot < live, weight, 0.0)
        projs[slot * weight.shape[0] : (slot + 1) * weight.shape[0]] = weight.astype(BF)

    def move(start, size):
        pieces = [flat(corr[spot, start : start + size]) for spot in spots]
        total = dot(jnp.concatenate(pieces, axis=1), projs[...])
        moved = jnp.maximum(total, 0.0).reshape(size, cols, hid)
        joined[start : start + size, main] = moved
        ext[MOT, HALO + start : HALO + start + size] = moved.astype(BF)

    move(0, HALO)
    move(rows - HALO, HALO)
    send_lat(MOT)
    for start in range(HALO, rows - HALO, HALO):
        move(start, HALO)
    send_lon(MOT, joined[:, 8:16], joined[:, cols : 8 + cols])
    for steps in evens:
        direct(steps).wait_send()
    for number, source in enumerate([0] + sources):
        forward(number, source).wait_send()
    inputs_lat(1, MOT, None, inner)
    receive_lon(MOT, joined)
    inputs_lon(1, None)
    receive_lat(MOT)
    inputs_lat(1, MOT, None, outer)
    loads[6].wait()
    loads[7].wait()

    def pass_lon(e, blocks):
        count = sum(size for _, size in blocks)

        def take(ref, *rest):
            parts = [ref[(slice(start, start + size),) + rest] for start, size in blocks]
            return joined_up(parts, 0)

        def put(ref, value, *rest, shift=0, lead=()):
            done = 0
            for start, size in blocks:
                at = slice(start + shift, start + shift + size)
                ref[lead + (at,) + rest] = value[done : done + size]
                done += size

        pieces = [flat(take(s_lon, slice(2 + k, 2 + k + near))).astype(BF) for k in range(5)]
        mixed = dot(jnp.concatenate(pieces, axis=1), zr_ref[0])
        shape = (count, near, hid)
        put(z_lon, sigmoid(take(xl_z) + mixed[:, :hid].reshape(shape)))
        reset = sigmoid(take(xl_r) + mixed[:, hid:].reshape(shape))
        put(rs_lon, reset * take(s_lon, slice(4, 4 + near)))
        pieces = [flat(take(rs_lon, slice(2 + k, 2 + k + cols))).astype(BF) for k in range(5)]
        mixed = dot(jnp.concatenate(pieces, axis=1), q_ref[0]).reshape(count, cols, hid)
        middle = slice(4, 4 + cols)
        candidate = jnp.tanh(take(xl_q, middle) + mixed)
        state = take(s_lon, main)
        state = state + take(z_lon, middle) * (candidate - state)
        put(s_lat, state)
        put(ext, state.astype(BF), shift=HALO, lead=(e,))

    def gates_lat(e, blocks, bands):
        wide = sum(band.stop - band.start for band in bands)

        def take(ref, lead, start, size):
            at = slice(start, start + size)
            return joined_up([ref[lead + (at, band)] for band in bands], 1)

        def put(ref, start, size, value):
            done = 0
            for band in bands:
                width = band.stop - band.start
                ref[start : start + size, band] = value[:, done : done + width]
                done += width

        pieces = [
            joined_up([flat(take(ext, (e,), start + k, size)) for start, size in blocks], 0)
            for k in range(5)
        ]
        mixed = dot(jnp.concatenate(pieces, axis=1), zr_ref[1])
        done = 0
        for start, size in blocks:
            shape = (size, wide, hid)
            part = mixed[done : done + size * wide]
            done += size * wide
            z = sigmoid(take(xt_z, (), start, size) + part[:, :hid].reshape(shape))
            put(z_lat, start, size, z)
            reset = sigmoid(take(xt_r, (), start, size) + part[:, hid:].reshape(shape))
            if start == 0:
                held = [take(ext, (e,), 2, 2).astype(F32), take(s_lat, (), 0, 2)]
            elif start + size == rows + 4:
                held = [take(s_lat, (), rows - 2, 2), take(ext, (e,), rows + HALO, 2).astype(F32)]
            else:
                held = [take(s_lat, (), start - 2, size)]
            put(rs_lat, start, size, (reset * joined_up(held, 0)).astype(BF))

    def update_lat(bands):
        wide = sum(band.stop - band.start for band in bands)

        def take(ref, start):
            return joined_up([ref[start : start + rows, band] for band in bands], 1)

        pieces = [flat(take(rs_lat, k)) for k in range(5)]
        mixed = dot(jnp.concatenate(pieces, axis=1), q_ref[1]).reshape(rows, wide, hid)
        candidate = jnp.tanh(take(xt_q, 2) + mixed)
        state = take(s_lat, 0)
        state = state + take(z_lat, 2) * (candidate - state)
        done = 0
        for band in bands:
            width = band.stop - band.start
            s_lon[:, 8 + band.start : 8 + band.stop] = state[:, done : done + width]
            done += width
        return state

    edges = (slice(0, 16), slice(cols - 16, cols))
    centre = (slice(16, cols - 16),)
    panel = (slice(0, cols),)

    def iteration(index, carry):
        e = STATE + index
        receive_lon(e, s_lon)
        pass_lon(e, ((0, HALO), (rows - HALO, HALO)))
        send_lat(e)
        pass_lon(e, ((HALO, rows - 2 * HALO),))
        gates_lat(e, ((4, rows - 4),), panel)
        receive_lat(e)
        gates_lat(e, outer, edges)
        state = update_lat(edges)

        @pl.when(index < ITERS - 1)
        def _():
            send_lon(e + 1, s_lon[:, 8:16], s_lon[:, cols : 8 + cols])

        gates_lat(e, outer, centre)
        update_lat(centre)
        return carry

    lax.fori_loop(0, ITERS, iteration, 0)
    out_ref[...] = s_lon[:, main].astype(BF)


def local(
    n_lat,
    n_lon,
    feat_one,
    feat_two,
    context_in,
    hidden_init,
    corr_proj,
    input_conv,
    state_zr,
    state_q,
    update_bias,
    gate_bias,
    blk_offset,
    blk_class,
    blk_count,
):
    rows, cols, chans = feat_one.shape
    hid = hidden_init.shape[2]
    points = POOLR * POOLC
    slots = blk_offset.shape[2]
    reach = min(n_lon, 2 * RMAX + 1)
    wide, near = cols + 16, cols + 8
    tall = rows + 2 * HALO
    count = STATE + ITERS
    taps = state_zr.shape[1]
    state_zr = state_zr.reshape(2, taps * hid, 2 * hid)
    state_q = state_q.reshape(2, taps * hid, hid)
    vmem = pl.BlockSpec(memory_space=pltpu.VMEM)
    smem = pl.BlockSpec(memory_space=pltpu.SMEM)
    hbm = pl.BlockSpec(memory_space=pl.ANY)
    held = (feat_one, feat_two, hidden_init, corr_proj, input_conv, state_zr, state_q)
    return pl.pallas_call(
        functools.partial(kernel, n_lat, n_lon),
        out_shape=jax.ShapeDtypeStruct((rows, cols, hid), BF),
        in_specs=[smem] * 3 + [hbm] * 8 + [vmem] * 2,
        out_specs=vmem,
        scratch_shapes=[pltpu.VMEM(value.shape, BF) for value in held]
        + [
            pltpu.VMEM((count, tall, cols, hid), BF),
            pltpu.VMEM((count, 2, rows // 2, 16, hid), BF),
            pltpu.VMEM((count, 2, rows // 2, 16, hid), BF),
            pltpu.VMEM((reach, points, chans), BF),
            pltpu.VMEM((reach, rows, cols, points), BF),
            pltpu.VMEM((slots * points, hid), BF),
            pltpu.VMEM((rows, wide, hid), F32),
            pltpu.VMEM((rows, near, hid), F32),
            pltpu.VMEM((rows, near, hid), F32),
            pltpu.VMEM((rows, near, hid), F32),
            pltpu.VMEM((rows + 4, cols, hid), F32),
            pltpu.VMEM((rows + 4, cols, hid), F32),
            pltpu.VMEM((rows + 4, cols, hid), F32),
            pltpu.VMEM((rows, wide, hid), F32),
            pltpu.VMEM((rows, cols, hid), F32),
            pltpu.VMEM((rows, near, hid), F32),
            pltpu.VMEM((rows + 4, cols, hid), BF),
            pltpu.VMEM((rows, near, hid), F32),
            pltpu.VMEM((rows + 4, cols, hid), F32),
            pltpu.SemaphoreType.DMA((8,)),
            pltpu.SemaphoreType.DMA((count, 2)),
            pltpu.SemaphoreType.DMA((count, 2)),
            pltpu.SemaphoreType.DMA((count, 2)),
            pltpu.SemaphoreType.DMA((count, 2)),
            pltpu.SemaphoreType.DMA((4,)),
            pltpu.SemaphoreType.DMA((reach,)),
            pltpu.SemaphoreType.DMA((4,)),
        ],
        compiler_params=pltpu.CompilerParams(
            collective_id=0, has_side_effects=True, vmem_limit_bytes=56 * 1024 * 1024
        ),
        name="refine",
    )(
        blk_offset,
        blk_class,
        blk_count,
        feat_one,
        feat_two,
        context_in,
        hidden_init,
        corr_proj,
        input_conv,
        state_zr,
        state_q,
        update_bias,
        gate_bias,
    )


def solution(mesh):
    placed = (
        P("lat", "lon", None),
        P("lat", "lon", None),
        P("lat", "lon", None),
        P("lat", "lon", None),
        P(),
        P(),
        P(),
        P(),
        P(),
        P(),
        P("lat", "lon", None),
        P("lat", "lon", None),
        P("lat", "lon"),
    )
    return jax.shard_map(
        functools.partial(local, mesh.shape["lat"], mesh.shape["lon"]),
        mesh=mesh,
        in_specs=placed,
        out_specs=P("lat", "lon", None),
        check_vma=False,
    )
```

```python
import functools

import jax
import jax.numpy as jnp
from jax import lax
from jax.experimental import pallas as pl
from jax.experimental.pallas import tpu as pltpu
from jax.sharding import PartitionSpec as P

POOLR = 8
POOLC = 16
RMAX = 4
ITERS = 4
HALO = 4
CTX, MOT, STATE = 0, 1, 2
MESH = pl.DeviceIdType.MESH
BF = jnp.bfloat16
F32 = jnp.float32


def sigmoid(value):
    return 0.5 * jnp.tanh(0.5 * value) + 0.5


def dot(left, right):
    return jnp.dot(left, right, preferred_element_type=F32)


def flat(value):
    return value.reshape(-1, value.shape[-1])


def joined_up(parts, axis):
    return parts[0] if len(parts) == 1 else jnp.concatenate(parts, axis=axis)


def kernel(
    n_lat,
    n_lon,
    offset_ref,
    class_ref,
    count_ref,
    one_hbm,
    two_hbm,
    ctx_hbm,
    init_hbm,
    proj_hbm,
    input_hbm,
    zr_hbm,
    q_hbm,
    ubias_ref,
    gbias_ref,
    out_ref,
    one_ref,
    two_ref,
    init_ref,
    proj_ref,
    input_ref,
    zr_ref,
    q_ref,
    ext,
    side_out,
    side_in,
    pool,
    corr,
    projs,
    joined,
    xl_z,
    xl_r,
    xl_q,
    xt_z,
    xt_r,
    xt_q,
    s_lon,
    s_lat,
    rs_lon,
    rs_lat,
    z_lon,
    z_lat,
    load_sem,
    ns_send,
    ns_recv,
    ew_send,
    ew_recv,
    pool_send,
    pool_recv,
    pass_send,
):
    rows, cols, chans = one_ref.shape
    hid = init_ref.shape[2]
    near = cols + 8
    slots = offset_ref.shape[2]
    lat, lon = lax.axis_index("lat"), lax.axis_index("lon")
    north, south = lax.rem(lat + n_lat - 1, n_lat), lax.rem(lat + 1, n_lat)
    west, east = lax.rem(lon + n_lon - 1, n_lon), lax.rem(lon + 1, n_lon)
    has_n, has_s = lat > 0, lat < n_lat - 1
    parity = lax.rem(lon, 2)
    lowest = -min(RMAX, (n_lon - 1) // 2)
    highest = min(RMAX, n_lon // 2)

    top = slice(HALO, 2 * HALO)
    bottom = slice(rows, rows + HALO)
    above = slice(0, HALO)
    below = slice(rows + HALO, rows + 2 * HALO)
    body = slice(HALO, HALO + rows)
    main = slice(8, 8 + cols)

    loads = [
        pltpu.make_async_copy(source, target, load_sem.at[number])
        for number, (source, target) in enumerate(
            (
                (two_hbm, two_ref),
                (ctx_hbm, ext.at[CTX, body]),
                (init_hbm, init_ref),
                (input_hbm, input_ref),
                (one_hbm, one_ref),
                (proj_hbm, proj_ref),
                (zr_hbm, zr_ref),
                (q_hbm, q_ref),
            )
        )
    ]
    for load in loads:
        load.start()

    def place(offset):
        return lax.rem(offset - lowest + n_lon, n_lon)

    def along(steps):
        return lax.rem(lon + steps + n_lon, n_lon)

    evens = [d for d in (2, -2, 4, -4) if lowest <= d <= highest]

    barrier = pltpu.get_barrier_semaphore()
    partners = [1, -1] + evens
    for steps in partners:
        pl.semaphore_signal(
            barrier, inc=1, device_id=(lat, along(steps)), device_id_type=MESH
        )

    @pl.when(has_n)
    def _():
        pl.semaphore_signal(barrier, inc=1, device_id=(north, lon), device_id_type=MESH)

    @pl.when(has_s)
    def _():
        pl.semaphore_signal(barrier, inc=1, device_id=(south, lon), device_id_type=MESH)

    left, right = slice(0, 16), slice(cols - 16, cols)
    bands = (left, right, slice(16, cols - 16))
    edges, centre, panel = (0, 1), (2,), (0, 1, 2)

    def to_lat(e, way, band):
        return pltpu.make_async_remote_copy(
            src_ref=ext.at[e, bottom if way else top, bands[band]],
            dst_ref=ext.at[e, above if way else below, bands[band]],
            send_sem=ns_send.at[e, way, band],
            recv_sem=ns_recv.at[e, way, band],
            device_id=(south if way else north, lon),
            device_id_type=MESH,
        )

    def to_lon(e, way):
        return pltpu.make_async_remote_copy(
            src_ref=side_out.at[e, way],
            dst_ref=side_in.at[e, 1 - way],
            send_sem=ew_send.at[e, way],
            recv_sem=ew_recv.at[e, way],
            device_id=(lat, east if way else west),
            device_id_type=MESH,
        )

    def send_lat(e, way, chosen=panel):
        @pl.when(has_s if way else has_n)
        def _():
            for band in chosen:
                to_lat(e, way, band).start()

    def receive_lat(e, chosen=panel):
        @pl.when(has_s)
        def _():
            for band in chosen:
                to_lat(e, 0, band).wait_recv()
                to_lat(e, 1, band).wait_send()

        @pl.when(has_n)
        def _():
            for band in chosen:
                to_lat(e, 1, band).wait_recv()
                to_lat(e, 0, band).wait_send()

    @pl.when(jnp.logical_not(has_s))
    def _():
        for e in range(ext.shape[0]):
            ext[e, below] = jnp.zeros((HALO, cols, hid), BF)

    @pl.when(jnp.logical_not(has_n))
    def _():
        for e in range(ext.shape[0]):
            ext[e, above] = jnp.zeros((HALO, cols, hid), BF)

    def send_lon(e, low, high):
        for way, value in enumerate((low, high)):
            side_out[e, way] = value.reshape(rows // 2, 16, hid).astype(BF)
        for way in range(2):
            to_lon(e, way).start()

    def receive_lon(e, target):
        for way in range(2):
            to_lon(e, way).wait()
        target[:, 0:8] = side_in[e, 0].astype(F32).reshape(rows, 8, hid)
        target[:, 8 + cols :] = side_in[e, 1].astype(F32).reshape(rows, 8, hid)

    def direct(steps):
        return pltpu.make_async_remote_copy(
            src_ref=pool.at[-lowest],
            dst_ref=pool.at[place(-steps)],
            send_sem=pool_send.at[evens.index(steps)],
            recv_sem=pool_recv.at[place(-steps)],
            device_id=(lat, along(steps)),
            device_id_type=MESH,
        )

    sibling = lon + 1 - 2 * parity

    def forward(number, source):
        target = source - 1 + 2 * parity
        return pltpu.make_async_remote_copy(
            src_ref=pool.at[place(source)],
            dst_ref=pool.at[place(target)],
            send_sem=pass_send.at[number],
            recv_sem=pool_recv.at[place(target)],
            device_id=(lat, sibling),
            device_id_type=MESH,
        )

    def arrived(spot):
        return pltpu.make_async_remote_copy(
            src_ref=pool.at[-lowest],
            dst_ref=pool.at[spot],
            send_sem=pool_send.at[0],
            recv_sem=pool_recv.at[spot],
            device_id=(lat, sibling),
            device_id_type=MESH,
        ).wait_recv()

    point = lax.broadcasted_iota(jnp.int32, (POOLC, 2 * cols), 0)
    cell = lax.rem(lax.broadcasted_iota(jnp.int32, (POOLC, 2 * cols), 1), cols)
    pool_rows, pool_cols = rows // POOLR, cols // POOLC
    inside = (cell >= point * pool_cols) & (cell < (point + 1) * pool_cols)
    window = jnp.where(inside, 1.0 / (pool_rows * pool_cols), 0.0).astype(BF)
    loads[0].wait()
    for index in range(POOLR):
        block = flat(two_ref[pool_rows * index : pool_rows * (index + 1)])
        pool[-lowest, POOLC * index : POOLC * (index + 1)] = dot(window, block).astype(BF)

    lat_partners = has_n.astype(jnp.int32) + has_s.astype(jnp.int32)
    pl.semaphore_wait(barrier, len(partners) + lat_partners)
    for steps in evens:
        direct(steps).start()
    forward(0, 0).start()
    loads[1].wait()
    send_lat(CTX, 0)
    send_lat(CTX, 1)
    whole = ext[CTX, body].astype(F32)
    joined[:, main] = whole
    send_lon(CTX, whole[:, 0:8], whole[:, cols - 8 :])
    loads[2].wait()
    whole = init_ref[...].astype(F32)
    s_lon[:, main] = whole
    send_lon(STATE, whole[:, 0:8], whole[:, cols - 8 :])

    def weights(index, part):
        channels = slice(part * hid, (part + 1) * hid)
        return jnp.concatenate([input_ref[index, tap, channels, :] for tap in range(5)], axis=0)

    def biases(index):
        gate = gbias_ref[index : index + 1]
        parts = ubias_ref[index : index + 1], gate[:, :hid], gate[:, hid:]
        return [part.reshape(1, 1, hid) for part in parts]

    def keep(stores, at, total, shape, base):
        for number, store in enumerate(stores):
            value = total[:, number * hid : (number + 1) * hid].reshape(shape)
            store[at] = value + (store[at] if base is None else base[number])

    def inputs_lon(part, base):
        weight = weights(0, part)
        step = rows // 2

        def chunk(index, carry):
            at = pl.ds(index * step, step)
            pieces = [flat(joined[at, 2 + k : 2 + k + near]).astype(BF) for k in range(5)]
            total = dot(jnp.concatenate(pieces, axis=1), weight)
            keep((xl_z, xl_r, xl_q), at, total, (step, near, hid), base)
            return carry

        lax.fori_loop(0, 2, chunk, 0)

    def inputs_lat(part, e, base, blocks):
        weight = weights(1, part)
        for start, size in blocks:
            pieces = [flat(ext[e, start + k : start + k + size]) for k in range(5)]
            total = dot(jnp.concatenate(pieces, axis=1), weight)
            at = slice(start, start + size)
            keep((xt_z, xt_r, xt_q), at, total, (size, cols, hid), base)

    inner = ((4, rows // 2 - 2), (rows // 2 + 2, rows // 2 - 2))
    outer = ((0, 4), (rows, 4))

    loads[3].wait()
    inputs_lat(0, CTX, biases(1), inner)
    sources = [-2, 2, 4 - 8 * parity]

    def hand_on(number):
        arrived(place(sources[number]))
        forward(number + 1, sources[number]).start()

    receive_lon(CTX, joined)
    hand_on(0)
    hand_on(1)
    inputs_lon(0, biases(0))
    hand_on(2)
    receive_lat(CTX)
    inputs_lat(0, CTX, biases(1), outer)

    scale = chans ** (-0.5)

    def correlate(*spots):
        keys = joined_up([pool[spot] for spot in spots], 0)
        points = pool.shape[1]
        step = rows // 4

        def chunk(index, carry):
            at = pl.ds(index * step, step)
            value = lax.dot_general(
                flat(one_ref[at]), keys, (((1,), (1,)), ((), ())), preferred_element_type=F32
            )
            value = (value * scale).astype(BF)
            for number, spot in enumerate(spots):
                part = value[:, number * points : (number + 1) * points]
                corr[spot, at] = part.reshape(step, cols, points)
            return carry

        lax.fori_loop(0, 4, chunk, 0)

    loads[4].wait()
    correlate(place(0), place(2))
    if n_lon > 2 * RMAX:
        arrived(place(4 * (2 * parity - 1)))
        correlate(place(-4))
    correlate(place(-2), place(4))
    for pair in ((-1, 1), (-3, 3)):
        for steps in pair:
            arrived(place(steps))
        correlate(*[place(steps) for steps in pair])

    loads[5].wait()
    live = count_ref[0, 0]
    spots = []
    for slot in range(slots):
        offset = offset_ref[0, 0, slot]
        spots.append(jnp.where(offset < lowest, offset + n_lon, offset) - lowest)
        weight = proj_ref[class_ref[0, 0, slot]].astype(F32)
        weight = jnp.where(slot < live, weight, 0.0)
        projs[slot * weight.shape[0] : (slot + 1) * weight.shape[0]] = weight.astype(BF)

    def move(chosen):
        step = rows // 2
        wide = sum(bands[band].stop - bands[band].start for band in chosen)

        def chunk(index, carry):
            start = index * step
            at = pl.ds(start, step)
            pieces = []
            for spot in spots:
                parts = [corr[spot, at, bands[band]] for band in chosen]
                pieces.append(flat(joined_up(parts, 1)))
            total = dot(jnp.concatenate(pieces, axis=1), projs[...])
            moved = jnp.maximum(total, 0.0).reshape(step, wide, hid)
            done = 0
            for band in chosen:
                low, high = bands[band].start, bands[band].stop
                part = moved[:, done : done + high - low]
                done += high - low
                joined[at, 8 + low : 8 + high] = part
                ext[MOT, pl.ds(HALO + start, step), bands[band]] = part.astype(BF)
            return carry

        lax.fori_loop(0, 2, chunk, 0)

    move(edges)
    send_lon(MOT, joined[:, 8:16], joined[:, cols : 8 + cols])
    move(centre)
    send_lat(MOT, 0)
    send_lat(MOT, 1)
    for steps in evens:
        direct(steps).wait_send()
    for number, source in enumerate([0] + sources):
        forward(number, source).wait_send()
    inputs_lat(1, MOT, None, inner)
    receive_lon(MOT, joined)
    inputs_lon(1, None)
    loads[6].wait()
    loads[7].wait()

    def pass_lon(e, blocks):
        count = sum(size for _, size in blocks)

        def take(ref, *rest):
            parts = [ref[(slice(start, start + size),) + rest] for start, size in blocks]
            return joined_up(parts, 0)

        def put(ref, value, *rest, shift=0, lead=()):
            done = 0
            for start, size in blocks:
                at = slice(start + shift, start + shift + size)
                ref[lead + (at,) + rest] = value[done : done + size]
                done += size

        pieces = [flat(take(s_lon, slice(2 + k, 2 + k + near))).astype(BF) for k in range(5)]
        mixed = dot(jnp.concatenate(pieces, axis=1), zr_ref[0])
        shape = (count, near, hid)
        put(z_lon, sigmoid(take(xl_z) + mixed[:, :hid].reshape(shape)))
        reset = sigmoid(take(xl_r) + mixed[:, hid:].reshape(shape))
        put(rs_lon, reset * take(s_lon, slice(4, 4 + near)))
        pieces = [flat(take(rs_lon, slice(2 + k, 2 + k + cols))).astype(BF) for k in range(5)]
        mixed = dot(jnp.concatenate(pieces, axis=1), q_ref[0]).reshape(count, cols, hid)
        middle = slice(4, 4 + cols)
        candidate = jnp.tanh(take(xl_q, middle) + mixed)
        state = take(s_lon, main)
        state = state + take(z_lon, middle) * (candidate - state)
        put(s_lat, state)
        put(ext, state.astype(BF), shift=HALO, lead=(e,))

    def gates_lat(e, blocks, chosen):
        spans = (slice(0, cols),) if chosen is panel else [bands[band] for band in chosen]
        wide = sum(band.stop - band.start for band in spans)

        def take(ref, lead, start, size):
            at = slice(start, start + size)
            return joined_up([ref[lead + (at, band)] for band in spans], 1)

        def put(ref, start, size, value):
            done = 0
            for band in spans:
                width = band.stop - band.start
                ref[start : start + size, band] = value[:, done : done + width]
                done += width

        pieces = [
            joined_up([flat(take(ext, (e,), start + k, size)) for start, size in blocks], 0)
            for k in range(5)
        ]
        mixed = dot(jnp.concatenate(pieces, axis=1), zr_ref[1])
        done = 0
        for start, size in blocks:
            shape = (size, wide, hid)
            part = mixed[done : done + size * wide]
            done += size * wide
            z = sigmoid(take(xt_z, (), start, size) + part[:, :hid].reshape(shape))
            put(z_lat, start, size, z)
            reset = sigmoid(take(xt_r, (), start, size) + part[:, hid:].reshape(shape))
            if start == 0:
                held = [take(ext, (e,), 2, 2).astype(F32), take(s_lat, (), 0, 2)]
            elif start + size == rows + 4:
                held = [take(s_lat, (), rows - 2, 2), take(ext, (e,), rows + HALO, 2).astype(F32)]
            else:
                held = [take(s_lat, (), start - 2, size)]
            put(rs_lat, start, size, (reset * joined_up(held, 0)).astype(BF))

    def update_lat(chosen):
        spans = [bands[band] for band in chosen]
        wide = sum(band.stop - band.start for band in spans)

        def take(ref, start):
            return joined_up([ref[start : start + rows, band] for band in spans], 1)

        pieces = [flat(take(rs_lat, k)) for k in range(5)]
        mixed = dot(jnp.concatenate(pieces, axis=1), q_ref[1]).reshape(rows, wide, hid)
        candidate = jnp.tanh(take(xt_q, 2) + mixed)
        state = take(s_lat, 0)
        state = state + take(z_lat, 2) * (candidate - state)
        done = 0
        for band in spans:
            width = band.stop - band.start
            s_lon[:, 8 + band.start : 8 + band.stop] = state[:, done : done + width]
            done += width

    def iteration(index, carry):
        e = STATE + index
        receive_lon(e, s_lon)
        pass_lon(e, ((0, HALO),))
        send_lat(e, 0, edges)
        pass_lon(e, ((rows - HALO, HALO),))
        send_lat(e, 1, edges)
        send_lat(e, 0, centre)
        send_lat(e, 1, centre)

        @pl.when(index == 0)
        def _():
            receive_lat(MOT)
            inputs_lat(1, MOT, None, outer)

        pass_lon(e, ((HALO, rows - 2 * HALO),))
        gates_lat(e, ((4, rows - 4),), panel)
        receive_lat(e, edges)
        gates_lat(e, outer, edges)
        update_lat(edges)

        @pl.when(index < ITERS - 1)
        def _():
            send_lon(e + 1, s_lon[:, 8:16], s_lon[:, cols : 8 + cols])

        receive_lat(e, centre)
        gates_lat(e, outer, centre)
        update_lat(centre)
        return carry

    lax.fori_loop(0, ITERS, iteration, 0)
    out_ref[...] = s_lon[:, main].astype(BF)


def local(
    n_lat,
    n_lon,
    feat_one,
    feat_two,
    context_in,
    hidden_init,
    corr_proj,
    input_conv,
    state_zr,
    state_q,
    update_bias,
    gate_bias,
    blk_offset,
    blk_class,
    blk_count,
):
    rows, cols, chans = feat_one.shape
    hid = hidden_init.shape[2]
    points = POOLR * POOLC
    slots = blk_offset.shape[2]
    reach = min(n_lon, 2 * RMAX + 1)
    wide, near = cols + 16, cols + 8
    tall = rows + 2 * HALO
    count = STATE + ITERS
    taps = state_zr.shape[1]
    state_zr = state_zr.reshape(2, taps * hid, 2 * hid)
    state_q = state_q.reshape(2, taps * hid, hid)
    vmem = pl.BlockSpec(memory_space=pltpu.VMEM)
    smem = pl.BlockSpec(memory_space=pltpu.SMEM)
    hbm = pl.BlockSpec(memory_space=pl.ANY)
    held = (feat_one, feat_two, hidden_init, corr_proj, input_conv, state_zr, state_q)
    return pl.pallas_call(
        functools.partial(kernel, n_lat, n_lon),
        out_shape=jax.ShapeDtypeStruct((rows, cols, hid), BF),
        in_specs=[smem] * 3 + [hbm] * 8 + [vmem] * 2,
        out_specs=vmem,
        scratch_shapes=[pltpu.VMEM(value.shape, BF) for value in held]
        + [
            pltpu.VMEM((count, tall, cols, hid), BF),
            pltpu.VMEM((count, 2, rows // 2, 16, hid), BF),
            pltpu.VMEM((count, 2, rows // 2, 16, hid), BF),
            pltpu.VMEM((reach, points, chans), BF),
            pltpu.VMEM((reach, rows, cols, points), BF),
            pltpu.VMEM((slots * points, hid), BF),
            pltpu.VMEM((rows, wide, hid), F32),
            pltpu.VMEM((rows, near, hid), F32),
            pltpu.VMEM((rows, near, hid), F32),
            pltpu.VMEM((rows, near, hid), F32),
            pltpu.VMEM((rows + 4, cols, hid), F32),
            pltpu.VMEM((rows + 4, cols, hid), F32),
            pltpu.VMEM((rows + 4, cols, hid), F32),
            pltpu.VMEM((rows, wide, hid), F32),
            pltpu.VMEM((rows, cols, hid), F32),
            pltpu.VMEM((rows, near, hid), F32),
            pltpu.VMEM((rows + 4, cols, hid), BF),
            pltpu.VMEM((rows, near, hid), F32),
            pltpu.VMEM((rows + 4, cols, hid), F32),
            pltpu.SemaphoreType.DMA((8,)),
            pltpu.SemaphoreType.DMA((count, 2, 3)),
            pltpu.SemaphoreType.DMA((count, 2, 3)),
            pltpu.SemaphoreType.DMA((count, 2)),
            pltpu.SemaphoreType.DMA((count, 2)),
            pltpu.SemaphoreType.DMA((4,)),
            pltpu.SemaphoreType.DMA((reach,)),
            pltpu.SemaphoreType.DMA((4,)),
        ],
        compiler_params=pltpu.CompilerParams(
            collective_id=0, has_side_effects=True, vmem_limit_bytes=56 * 1024 * 1024
        ),
        name="refine",
    )(
        blk_offset,
        blk_class,
        blk_count,
        feat_one,
        feat_two,
        context_in,
        hidden_init,
        corr_proj,
        input_conv,
        state_zr,
        state_q,
        update_bias,
        gate_bias,
    )


def solution(mesh):
    placed = (
        P("lat", "lon", None),
        P("lat", "lon", None),
        P("lat", "lon", None),
        P("lat", "lon", None),
        P(),
        P(),
        P(),
        P(),
        P(),
        P(),
        P("lat", "lon", None),
        P("lat", "lon", None),
        P("lat", "lon"),
    )
    return jax.shard_map(
        functools.partial(local, mesh.shape["lat"], mesh.shape["lon"]),
        mesh=mesh,
        in_specs=placed,
        out_specs=P("lat", "lon", None),
        check_vma=False,
    )
```

```python
import functools

import jax
import jax.numpy as jnp
from jax import lax
from jax.experimental import pallas as pl
from jax.experimental.pallas import tpu as pltpu
from jax.sharding import PartitionSpec as P

POOLR = 8
POOLC = 16
RMAX = 4
ITERS = 4
HALO = 4
CTX, MOT, STATE = 0, 1, 2
MESH = pl.DeviceIdType.MESH
BF = jnp.bfloat16
F32 = jnp.float32


def sigmoid(value):
    return 0.5 * jnp.tanh(0.5 * value) + 0.5


def dot(left, right):
    return jnp.dot(left, right, preferred_element_type=F32)


def flat(value):
    return value.reshape(-1, value.shape[-1])


def joined_up(parts, axis):
    return parts[0] if len(parts) == 1 else jnp.concatenate(parts, axis=axis)


def kernel(
    n_lat,
    n_lon,
    offset_ref,
    class_ref,
    count_ref,
    one_hbm,
    two_hbm,
    ctx_hbm,
    init_hbm,
    proj_hbm,
    input_hbm,
    zr_hbm,
    q_hbm,
    ubias_ref,
    gbias_ref,
    out_ref,
    one_ref,
    two_ref,
    init_ref,
    proj_ref,
    input_ref,
    zr_ref,
    q_ref,
    ext,
    turned,
    pool,
    corr,
    projs,
    turn,
    xl_z,
    xl_r,
    xl_q,
    xt_z,
    xt_r,
    xt_q,
    s_lon,
    s_lat,
    rs_lon,
    rs_lat,
    z_lon,
    z_lat,
    load_sem,
    ns_send,
    ns_recv,
    ew_send,
    ew_recv,
    pool_send,
    pool_recv,
    pass_send,
):
    rows, cols, chans = one_ref.shape
    hid = init_ref.shape[2]
    near = cols + 4
    slots = offset_ref.shape[2]
    lat, lon = lax.axis_index("lat"), lax.axis_index("lon")
    north, south = lax.rem(lat + n_lat - 1, n_lat), lax.rem(lat + 1, n_lat)
    west, east = lax.rem(lon + n_lon - 1, n_lon), lax.rem(lon + 1, n_lon)
    has_n, has_s = lat > 0, lat < n_lat - 1
    parity = lax.rem(lon, 2)
    lowest = -min(RMAX, (n_lon - 1) // 2)
    highest = min(RMAX, n_lon // 2)

    top = slice(HALO, 2 * HALO)
    bottom = slice(rows, rows + HALO)
    above = slice(0, HALO)
    below = slice(rows + HALO, rows + 2 * HALO)
    body = slice(HALO, HALO + rows)

    loads = [
        pltpu.make_async_copy(source, target, load_sem.at[number])
        for number, (source, target) in enumerate(
            (
                (two_hbm, two_ref),
                (ctx_hbm, ext.at[CTX, body]),
                (init_hbm, init_ref),
                (input_hbm, input_ref),
                (one_hbm, one_ref),
                (proj_hbm, proj_ref),
                (zr_hbm, zr_ref),
                (q_hbm, q_ref),
            )
        )
    ]
    for load in loads:
        load.start()

    def place(offset):
        return lax.rem(offset - lowest + n_lon, n_lon)

    def along(steps):
        return lax.rem(lon + steps + n_lon, n_lon)

    evens = [d for d in (2, -2, 4, -4) if lowest <= d <= highest]

    barrier = pltpu.get_barrier_semaphore()
    partners = [1, -1] + evens
    for steps in partners:
        pl.semaphore_signal(
            barrier, inc=1, device_id=(lat, along(steps)), device_id_type=MESH
        )

    @pl.when(has_n)
    def _():
        pl.semaphore_signal(barrier, inc=1, device_id=(north, lon), device_id_type=MESH)

    @pl.when(has_s)
    def _():
        pl.semaphore_signal(barrier, inc=1, device_id=(south, lon), device_id_type=MESH)

    left, right = slice(0, 16), slice(cols - 16, cols)
    bands = (left, right, slice(16, cols - 16))
    edges, centre, panel = (0, 1), (2,), (0, 1, 2)

    def to_lat(e, way, band):
        return pltpu.make_async_remote_copy(
            src_ref=ext.at[e, bottom if way else top, bands[band]],
            dst_ref=ext.at[e, above if way else below, bands[band]],
            send_sem=ns_send.at[e, way, band],
            recv_sem=ns_recv.at[e, way, band],
            device_id=(south if way else north, lon),
            device_id_type=MESH,
        )

    def to_lon(e, way):
        return pltpu.make_async_remote_copy(
            src_ref=turned.at[e, cols : cols + HALO] if way else turned.at[e, HALO : 2 * HALO],
            dst_ref=turned.at[e, 0:HALO] if way else turned.at[e, cols + HALO :],
            send_sem=ew_send.at[e, way],
            recv_sem=ew_recv.at[e, way],
            device_id=(lat, east if way else west),
            device_id_type=MESH,
        )

    def send_lat(e, way, chosen=panel):
        @pl.when(has_s if way else has_n)
        def _():
            for band in chosen:
                to_lat(e, way, band).start()

    def receive_lat(e, chosen=panel):
        @pl.when(has_s)
        def _():
            for band in chosen:
                to_lat(e, 0, band).wait_recv()
                to_lat(e, 1, band).wait_send()

        @pl.when(has_n)
        def _():
            for band in chosen:
                to_lat(e, 1, band).wait_recv()
                to_lat(e, 0, band).wait_send()

    @pl.when(jnp.logical_not(has_s))
    def _():
        for e in range(ext.shape[0]):
            ext[e, below] = jnp.zeros((HALO, cols, hid), BF)

    @pl.when(jnp.logical_not(has_n))
    def _():
        for e in range(ext.shape[0]):
            ext[e, above] = jnp.zeros((HALO, cols, hid), BF)

    def send_lon(e):
        for way in range(2):
            to_lon(e, way).start()

    def receive_lon(e):
        for way in range(2):
            to_lon(e, way).wait()

    def turn_rows(value, band, target, first=0):
        low, high = band.start, band.stop
        for row in range(value.shape[0]):
            target[pl.ds(low * rows + first + row, high - low, stride=rows), :] = value[row]

    def cast_columns(source, band, e):
        low, high = band.start, band.stop
        value = source[low * rows : high * rows, :].astype(BF).reshape(high - low, rows, hid)
        turned[e, HALO + low : HALO + high] = value

    def direct(steps):
        return pltpu.make_async_remote_copy(
            src_ref=pool.at[-lowest],
            dst_ref=pool.at[place(-steps)],
            send_sem=pool_send.at[evens.index(steps)],
            recv_sem=pool_recv.at[place(-steps)],
            device_id=(lat, along(steps)),
            device_id_type=MESH,
        )

    sibling = lon + 1 - 2 * parity

    def forward(number, source):
        target = source - 1 + 2 * parity
        return pltpu.make_async_remote_copy(
            src_ref=pool.at[place(source)],
            dst_ref=pool.at[place(target)],
            send_sem=pass_send.at[number],
            recv_sem=pool_recv.at[place(target)],
            device_id=(lat, sibling),
            device_id_type=MESH,
        )

    def arrived(spot):
        return pltpu.make_async_remote_copy(
            src_ref=pool.at[-lowest],
            dst_ref=pool.at[spot],
            send_sem=pool_send.at[0],
            recv_sem=pool_recv.at[spot],
            device_id=(lat, sibling),
            device_id_type=MESH,
        ).wait_recv()

    point = lax.broadcasted_iota(jnp.int32, (POOLC, 2 * cols), 0)
    cell = lax.rem(lax.broadcasted_iota(jnp.int32, (POOLC, 2 * cols), 1), cols)
    pool_rows, pool_cols = rows // POOLR, cols // POOLC
    inside = (cell >= point * pool_cols) & (cell < (point + 1) * pool_cols)
    window = jnp.where(inside, 1.0 / (pool_rows * pool_cols), 0.0).astype(BF)
    loads[0].wait()
    for index in range(POOLR):
        block = flat(two_ref[pool_rows * index : pool_rows * (index + 1)])
        pool[-lowest, POOLC * index : POOLC * (index + 1)] = dot(window, block).astype(BF)

    lat_partners = has_n.astype(jnp.int32) + has_s.astype(jnp.int32)
    pl.semaphore_wait(barrier, len(partners) + lat_partners)
    for steps in evens:
        direct(steps).start()
    forward(0, 0).start()
    loads[1].wait()
    send_lat(CTX, 0)
    send_lat(CTX, 1)
    every = slice(0, cols)
    turn_rows(ext[CTX, body].astype(F32), every, turn)
    cast_columns(turn, every, CTX)
    send_lon(CTX)
    loads[2].wait()
    turn_rows(init_ref[...].astype(F32), every, s_lon)
    cast_columns(s_lon, every, STATE)
    send_lon(STATE)

    def weights(index, part):
        channels = slice(part * hid, (part + 1) * hid)
        return jnp.concatenate([input_ref[index, tap, channels, :] for tap in range(5)], axis=0)

    def biases(index):
        gate = gbias_ref[index : index + 1]
        parts = ubias_ref[index : index + 1], gate[:, :hid], gate[:, hid:]
        return [part.reshape(1, 1, hid) for part in parts]

    def keep(stores, at, total, shape, base):
        for number, store in enumerate(stores):
            value = total[:, number * hid : (number + 1) * hid].reshape(shape)
            store[at] = value + (store[at] if base is None else base[number])

    def inputs_lon(part, e, base):
        weight = weights(0, part)
        step = near // 2

        def chunk(index, carry):
            start = index * step
            pieces = [flat(turned[e, pl.ds(start + k, step)]) for k in range(5)]
            total = dot(jnp.concatenate(pieces, axis=1), weight)
            keep((xl_z, xl_r, xl_q), pl.ds(start, step), total, (step, rows, hid), base)
            return carry

        lax.fori_loop(0, 2, chunk, 0)

    def inputs_lat(part, e, base, blocks):
        weight = weights(1, part)
        for start, size in blocks:
            pieces = [flat(ext[e, start + k : start + k + size]) for k in range(5)]
            total = dot(jnp.concatenate(pieces, axis=1), weight)
            at = slice(start, start + size)
            keep((xt_z, xt_r, xt_q), at, total, (size, cols, hid), base)

    inner = ((4, rows // 2 - 2), (rows // 2 + 2, rows // 2 - 2))
    outer = ((0, 4), (rows, 4))

    loads[3].wait()
    inputs_lat(0, CTX, biases(1), inner)
    sources = [-2, 2, 4 - 8 * parity]

    def hand_on(number):
        arrived(place(sources[number]))
        forward(number + 1, sources[number]).start()

    receive_lon(CTX)
    hand_on(0)
    hand_on(1)
    inputs_lon(0, CTX, biases(0))
    hand_on(2)
    receive_lat(CTX)
    inputs_lat(0, CTX, biases(1), outer)

    scale = chans ** (-0.5)

    def correlate(*spots):
        keys = joined_up([pool[spot] for spot in spots], 0)
        points = pool.shape[1]
        step = rows // 4

        def chunk(index, carry):
            at = pl.ds(index * step, step)
            value = lax.dot_general(
                flat(one_ref[at]), keys, (((1,), (1,)), ((), ())), preferred_element_type=F32
            )
            value = (value * scale).astype(BF)
            for number, spot in enumerate(spots):
                part = value[:, number * points : (number + 1) * points]
                corr[spot, at] = part.reshape(step, cols, points)
            return carry

        lax.fori_loop(0, 4, chunk, 0)

    loads[4].wait()
    correlate(place(0), place(2))
    if n_lon > 2 * RMAX:
        arrived(place(4 * (2 * parity - 1)))
        correlate(place(-4))
    correlate(place(-2), place(4))
    for pair in ((-1, 1), (-3, 3)):
        for steps in pair:
            arrived(place(steps))
        correlate(*[place(steps) for steps in pair])

    loads[5].wait()
    live = count_ref[0, 0]
    spots = []
    for slot in range(slots):
        offset = offset_ref[0, 0, slot]
        spots.append(jnp.where(offset < lowest, offset + n_lon, offset) - lowest)
        weight = proj_ref[class_ref[0, 0, slot]].astype(F32)
        weight = jnp.where(slot < live, weight, 0.0)
        projs[slot * weight.shape[0] : (slot + 1) * weight.shape[0]] = weight.astype(BF)

    def move(chosen):
        step = rows // 2
        wide = sum(bands[band].stop - bands[band].start for band in chosen)

        for start in range(0, rows, step):
            at = slice(start, start + step)
            pieces = []
            for spot in spots:
                parts = [corr[spot, at, bands[band]] for band in chosen]
                pieces.append(flat(joined_up(parts, 1)))
            total = dot(jnp.concatenate(pieces, axis=1), projs[...])
            moved = jnp.maximum(total, 0.0).reshape(step, wide, hid)
            done = 0
            for band in chosen:
                low, high = bands[band].start, bands[band].stop
                part = moved[:, done : done + high - low]
                done += high - low
                turn_rows(part, bands[band], turn, start)
                ext[MOT, HALO + start : HALO + start + step, bands[band]] = part.astype(BF)
        for band in chosen:
            cast_columns(turn, bands[band], MOT)

    move(edges)
    send_lon(MOT)
    move(centre)
    send_lat(MOT, 0)
    send_lat(MOT, 1)
    for steps in evens:
        direct(steps).wait_send()
    for number, source in enumerate([0] + sources):
        forward(number, source).wait_send()
    inputs_lat(1, MOT, None, inner)
    receive_lon(MOT)
    inputs_lon(1, MOT, None)
    loads[6].wait()
    loads[7].wait()

    def gates_lon(e, blocks):
        pieces = [
            joined_up([flat(turned[e, start + k : start + k + size]) for start, size in blocks], 0)
            for k in range(5)
        ]
        mixed = dot(jnp.concatenate(pieces, axis=1), zr_ref[0])
        done = 0
        for start, size in blocks:
            at = slice(start, start + size)
            shape = (size, rows, hid)
            part = mixed[done : done + size * rows]
            done += size * rows
            z_lon[at] = sigmoid(xl_z[at] + part[:, :hid].reshape(shape))
            reset = sigmoid(xl_r[at] + part[:, hid:].reshape(shape))
            low, high = max(start, 2), min(start + size, cols + 2)
            held = []
            if start < 2:
                held.append(turned[e, 2:HALO].astype(F32))
            held.append(s_lon[(low - 2) * rows : (high - 2) * rows, :].reshape(-1, rows, hid))
            if start + size > cols + 2:
                held.append(turned[e, cols + HALO : cols + HALO + 2].astype(F32))
            rs_lon[at] = (reset * joined_up(held, 0)).astype(BF)

    def update_lon(e, chosen):
        spans = [bands[band] for band in chosen]

        def take(ref, shift):
            parts = [ref[span.start + shift : span.stop + shift] for span in spans]
            return flat(joined_up(parts, 0))

        pieces = [take(rs_lon, k) for k in range(5)]
        mixed = dot(jnp.concatenate(pieces, axis=1), q_ref[0])
        candidate = jnp.tanh(take(xl_q, 2) + mixed)
        state = joined_up([s_lon[span.start * rows : span.stop * rows, :] for span in spans], 0)
        state = state + take(z_lon, 2) * (candidate - state)
        done = 0
        for span in spans:
            for column in range(span.start, span.stop):
                part = state[done * rows : (done + 1) * rows]
                s_lat[pl.ds(column, rows, stride=cols), :] = part
                done += 1
        for span in spans:
            for row in range(rows):
                part = s_lat[row * cols + span.start : row * cols + span.stop, :]
                ext[e, HALO + row, span] = part.astype(BF)

    def state_rows(spans, start, size):
        parts = [
            s_lat[row * cols + span.start : row * cols + span.stop, :]
            for row in range(start, start + size)
            for span in spans
        ]
        return joined_up(parts, 0).reshape(size, -1, hid)

    def gates_lat(e, blocks, chosen):
        spans = (slice(0, cols),) if chosen is panel else [bands[band] for band in chosen]
        wide = sum(band.stop - band.start for band in spans)

        def take(ref, lead, start, size):
            at = slice(start, start + size)
            return joined_up([ref[lead + (at, band)] for band in spans], 1)

        def put(ref, start, size, value):
            done = 0
            for band in spans:
                width = band.stop - band.start
                ref[start : start + size, band] = value[:, done : done + width]
                done += width

        pieces = [
            joined_up([flat(take(ext, (e,), start + k, size)) for start, size in blocks], 0)
            for k in range(5)
        ]
        mixed = dot(jnp.concatenate(pieces, axis=1), zr_ref[1])
        done = 0
        for start, size in blocks:
            shape = (size, wide, hid)
            part = mixed[done : done + size * wide]
            done += size * wide
            z = sigmoid(take(xt_z, (), start, size) + part[:, :hid].reshape(shape))
            put(z_lat, start, size, z)
            reset = sigmoid(take(xt_r, (), start, size) + part[:, hid:].reshape(shape))
            if start == 0:
                held = [take(ext, (e,), 2, 2).astype(F32), state_rows(spans, 0, 2)]
            elif start + size == rows + 4:
                held = [state_rows(spans, rows - 2, 2), take(ext, (e,), rows + HALO, 2).astype(F32)]
            else:
                held = [state_rows(spans, start - 2, size)]
            put(rs_lat, start, size, (reset * joined_up(held, 0)).astype(BF))

    def update_lat(e, chosen):
        spans = [bands[band] for band in chosen]
        wide = sum(band.stop - band.start for band in spans)

        def take(ref, start):
            return joined_up([ref[start : start + rows, band] for band in spans], 1)

        pieces = [flat(take(rs_lat, k)) for k in range(5)]
        mixed = dot(jnp.concatenate(pieces, axis=1), q_ref[1]).reshape(rows, wide, hid)
        candidate = jnp.tanh(take(xt_q, 2) + mixed)
        state = state_rows(spans, 0, rows)
        state = state + take(z_lat, 2) * (candidate - state)
        done = 0
        for band in spans:
            width = band.stop - band.start
            part = state[:, done : done + width]
            out_ref[:, band] = part
            turn_rows(part, band, s_lon)
            cast_columns(s_lon, band, e + 1)
            done += width

    def iteration(index, carry):
        e = STATE + index
        gates_lon(e, ((4, cols - 4),))
        receive_lon(e)
        gates_lon(e, ((0, 4), (cols, 4)))
        update_lon(e, edges)
        send_lat(e, 0, edges)
        send_lat(e, 1, edges)
        update_lon(e, centre)
        send_lat(e, 0, centre)
        send_lat(e, 1, centre)

        @pl.when(index == 0)
        def _():
            receive_lat(MOT)
            inputs_lat(1, MOT, None, outer)

        gates_lat(e, ((4, rows - 4),), panel)
        receive_lat(e, edges)
        gates_lat(e, outer, edges)
        update_lat(e, edges)

        @pl.when(index < ITERS - 1)
        def _():
            send_lon(e + 1)

        receive_lat(e, centre)
        gates_lat(e, outer, centre)
        update_lat(e, centre)
        return carry

    lax.fori_loop(0, ITERS, iteration, 0)


def local(
    n_lat,
    n_lon,
    feat_one,
    feat_two,
    context_in,
    hidden_init,
    corr_proj,
    input_conv,
    state_zr,
    state_q,
    update_bias,
    gate_bias,
    blk_offset,
    blk_class,
    blk_count,
):
    rows, cols, chans = feat_one.shape
    hid = hidden_init.shape[2]
    points = POOLR * POOLC
    slots = blk_offset.shape[2]
    reach = min(n_lon, 2 * RMAX + 1)
    near = cols + 4
    tall = rows + 2 * HALO
    count = STATE + ITERS
    taps = state_zr.shape[1]
    state_zr = state_zr.reshape(2, taps * hid, 2 * hid)
    state_q = state_q.reshape(2, taps * hid, hid)
    vmem = pl.BlockSpec(memory_space=pltpu.VMEM)
    smem = pl.BlockSpec(memory_space=pltpu.SMEM)
    hbm = pl.BlockSpec(memory_space=pl.ANY)
    held = (feat_one, feat_two, hidden_init, corr_proj, input_conv, state_zr, state_q)
    hidden = pl.pallas_call(
        functools.partial(kernel, n_lat, n_lon),
        out_shape=jax.ShapeDtypeStruct((rows, cols, hid), F32),
        in_specs=[smem] * 3 + [hbm] * 8 + [vmem] * 2,
        out_specs=vmem,
        scratch_shapes=[pltpu.VMEM(value.shape, BF) for value in held]
        + [
            pltpu.VMEM((count, tall, cols, hid), BF),
            pltpu.VMEM((count + 1, cols + 2 * HALO, rows, hid), BF),
            pltpu.VMEM((reach, points, chans), BF),
            pltpu.VMEM((reach, rows, cols, points), BF),
            pltpu.VMEM((slots * points, hid), BF),
            pltpu.VMEM((cols * rows, hid), F32),
            pltpu.VMEM((near, rows, hid), F32),
            pltpu.VMEM((near, rows, hid), F32),
            pltpu.VMEM((near, rows, hid), F32),
            pltpu.VMEM((rows + 4, cols, hid), F32),
            pltpu.VMEM((rows + 4, cols, hid), F32),
            pltpu.VMEM((rows + 4, cols, hid), F32),
            pltpu.VMEM((cols * rows, hid), F32),
            pltpu.VMEM((rows * cols, hid), F32),
            pltpu.VMEM((near, rows, hid), BF),
            pltpu.VMEM((rows + 4, cols, hid), BF),
            pltpu.VMEM((near, rows, hid), F32),
            pltpu.VMEM((rows + 4, cols, hid), F32),
            pltpu.SemaphoreType.DMA((8,)),
            pltpu.SemaphoreType.DMA((count, 2, 3)),
            pltpu.SemaphoreType.DMA((count, 2, 3)),
            pltpu.SemaphoreType.DMA((count, 2)),
            pltpu.SemaphoreType.DMA((count, 2)),
            pltpu.SemaphoreType.DMA((4,)),
            pltpu.SemaphoreType.DMA((reach,)),
            pltpu.SemaphoreType.DMA((4,)),
        ],
        compiler_params=pltpu.CompilerParams(
            collective_id=0, has_side_effects=True, vmem_limit_bytes=56 * 1024 * 1024
        ),
        name="refine",
    )(
        blk_offset,
        blk_class,
        blk_count,
        feat_one,
        feat_two,
        context_in,
        hidden_init,
        corr_proj,
        input_conv,
        state_zr,
        state_q,
        update_bias,
        gate_bias,
    )
    return hidden.astype(BF)


def solution(mesh):
    placed = (
        P("lat", "lon", None),
        P("lat", "lon", None),
        P("lat", "lon", None),
        P("lat", "lon", None),
        P(),
        P(),
        P(),
        P(),
        P(),
        P(),
        P("lat", "lon", None),
        P("lat", "lon", None),
        P("lat", "lon"),
    )
    return jax.shard_map(
        functools.partial(local, mesh.shape["lat"], mesh.shape["lon"]),
        mesh=mesh,
        in_specs=placed,
        out_specs=P("lat", "lon", None),
        check_vma=False,
    )
```

```python
import functools

import jax
import jax.numpy as jnp
from jax import lax
from jax.experimental import pallas as pl
from jax.experimental.pallas import tpu as pltpu
from jax.sharding import PartitionSpec as P

POOLR = 8
POOLC = 16
RMAX = 4
ITERS = 4
HALO = 4
CTX, MOT, STATE = 0, 1, 2
MESH = pl.DeviceIdType.MESH
BF = jnp.bfloat16
F32 = jnp.float32


def sigmoid(value):
    return 0.5 * jnp.tanh(0.5 * value) + 0.5


def dot(left, right):
    return jnp.dot(left, right, preferred_element_type=F32)


def flat(value):
    return value.reshape(-1, value.shape[-1])


def joined_up(parts, axis):
    return parts[0] if len(parts) == 1 else jnp.concatenate(parts, axis=axis)


def kernel(
    n_lat,
    n_lon,
    offset_ref,
    class_ref,
    count_ref,
    one_hbm,
    two_hbm,
    ctx_hbm,
    init_hbm,
    proj_hbm,
    input_hbm,
    zr_hbm,
    q_hbm,
    ubias_ref,
    gbias_ref,
    out_ref,
    one_ref,
    two_ref,
    init_ref,
    proj_ref,
    input_ref,
    zr_ref,
    q_ref,
    ext,
    turned,
    pool,
    corr,
    projs,
    turn,
    xl_z,
    xl_r,
    xl_q,
    xt_z,
    xt_r,
    xt_q,
    s_lon,
    s_lat,
    rs_lon,
    rs_lat,
    z_lon,
    z_lat,
    load_sem,
    ns_send,
    ns_recv,
    ew_send,
    ew_recv,
    pool_send,
    pool_recv,
    pass_send,
):
    rows, cols, chans = one_ref.shape
    hid = init_ref.shape[2]
    near = cols + 4
    slots = offset_ref.shape[2]
    lat, lon = lax.axis_index("lat"), lax.axis_index("lon")
    north, south = lax.rem(lat + n_lat - 1, n_lat), lax.rem(lat + 1, n_lat)
    west, east = lax.rem(lon + n_lon - 1, n_lon), lax.rem(lon + 1, n_lon)
    has_n, has_s = lat > 0, lat < n_lat - 1
    parity = lax.rem(lon, 2)
    lowest = -min(RMAX, (n_lon - 1) // 2)
    highest = min(RMAX, n_lon // 2)

    top = slice(HALO, 2 * HALO)
    bottom = slice(rows, rows + HALO)
    above = slice(0, HALO)
    below = slice(rows + HALO, rows + 2 * HALO)
    body = slice(HALO, HALO + rows)

    loads = [
        pltpu.make_async_copy(source, target, load_sem.at[number])
        for number, (source, target) in enumerate(
            (
                (two_hbm, two_ref),
                (ctx_hbm, ext.at[CTX, body]),
                (init_hbm, init_ref),
                (input_hbm, input_ref),
                (one_hbm, one_ref),
                (proj_hbm, proj_ref),
                (zr_hbm, zr_ref),
                (q_hbm, q_ref),
            )
        )
    ]
    for load in loads:
        load.start()

    def place(offset):
        return lax.rem(offset - lowest + n_lon, n_lon)

    def along(steps):
        return lax.rem(lon + steps + n_lon, n_lon)

    evens = [d for d in (2, -2, 4, -4) if lowest <= d <= highest]

    barrier = pltpu.get_barrier_semaphore()
    partners = [1, -1] + evens
    for steps in partners:
        pl.semaphore_signal(
            barrier, inc=1, device_id=(lat, along(steps)), device_id_type=MESH
        )

    @pl.when(has_n)
    def _():
        pl.semaphore_signal(barrier, inc=1, device_id=(north, lon), device_id_type=MESH)

    @pl.when(has_s)
    def _():
        pl.semaphore_signal(barrier, inc=1, device_id=(south, lon), device_id_type=MESH)

    left, right = slice(0, 16), slice(cols - 16, cols)
    bands = (left, right, slice(16, cols - 16))
    edges, centre, panel = (0, 1), (2,), (0, 1, 2)

    def to_lat(e, way, band):
        return pltpu.make_async_remote_copy(
            src_ref=ext.at[e, bottom if way else top, bands[band]],
            dst_ref=ext.at[e, above if way else below, bands[band]],
            send_sem=ns_send.at[e, way, band],
            recv_sem=ns_recv.at[e, way, band],
            device_id=(south if way else north, lon),
            device_id_type=MESH,
        )

    def to_lon(e, way):
        return pltpu.make_async_remote_copy(
            src_ref=turned.at[e, cols : cols + HALO] if way else turned.at[e, HALO : 2 * HALO],
            dst_ref=turned.at[e, 0:HALO] if way else turned.at[e, cols + HALO :],
            send_sem=ew_send.at[e, way],
            recv_sem=ew_recv.at[e, way],
            device_id=(lat, east if way else west),
            device_id_type=MESH,
        )

    def send_lat(e, way, chosen=panel):
        @pl.when(has_s if way else has_n)
        def _():
            for band in chosen:
                to_lat(e, way, band).start()

    def receive_lat(e, chosen=panel):
        @pl.when(has_s)
        def _():
            for band in chosen:
                to_lat(e, 0, band).wait_recv()
                to_lat(e, 1, band).wait_send()

        @pl.when(has_n)
        def _():
            for band in chosen:
                to_lat(e, 1, band).wait_recv()
                to_lat(e, 0, band).wait_send()

    @pl.when(jnp.logical_not(has_s))
    def _():
        for e in range(ext.shape[0]):
            ext[e, below] = jnp.zeros((HALO, cols, hid), BF)

    @pl.when(jnp.logical_not(has_n))
    def _():
        for e in range(ext.shape[0]):
            ext[e, above] = jnp.zeros((HALO, cols, hid), BF)

    def send_lon(e):
        for way in range(2):
            to_lon(e, way).start()

    def receive_lon(e):
        for way in range(2):
            to_lon(e, way).wait()

    def turn_rows(value, band, target, first=0):
        low, high = band.start, band.stop
        for row in range(value.shape[0]):
            target[pl.ds(low * rows + first + row, high - low, stride=rows), :] = value[row]

    def cast_columns(source, band, e):
        low, high = band.start, band.stop
        value = source[low * rows : high * rows, :].astype(BF).reshape(high - low, rows, hid)
        turned[e, HALO + low : HALO + high] = value

    def direct(steps):
        return pltpu.make_async_remote_copy(
            src_ref=pool.at[-lowest],
            dst_ref=pool.at[place(-steps)],
            send_sem=pool_send.at[evens.index(steps)],
            recv_sem=pool_recv.at[place(-steps)],
            device_id=(lat, along(steps)),
            device_id_type=MESH,
        )

    sibling = lon + 1 - 2 * parity

    def forward(number, source):
        target = source - 1 + 2 * parity
        return pltpu.make_async_remote_copy(
            src_ref=pool.at[place(source)],
            dst_ref=pool.at[place(target)],
            send_sem=pass_send.at[number],
            recv_sem=pool_recv.at[place(target)],
            device_id=(lat, sibling),
            device_id_type=MESH,
        )

    def arrived(spot):
        return pltpu.make_async_remote_copy(
            src_ref=pool.at[-lowest],
            dst_ref=pool.at[spot],
            send_sem=pool_send.at[0],
            recv_sem=pool_recv.at[spot],
            device_id=(lat, sibling),
            device_id_type=MESH,
        ).wait_recv()

    point = lax.broadcasted_iota(jnp.int32, (POOLC, 2 * cols), 0)
    cell = lax.rem(lax.broadcasted_iota(jnp.int32, (POOLC, 2 * cols), 1), cols)
    pool_rows, pool_cols = rows // POOLR, cols // POOLC
    inside = (cell >= point * pool_cols) & (cell < (point + 1) * pool_cols)
    window = jnp.where(inside, 1.0 / (pool_rows * pool_cols), 0.0).astype(BF)
    loads[0].wait()
    for index in range(POOLR):
        block = flat(two_ref[pool_rows * index : pool_rows * (index + 1)])
        pool[-lowest, POOLC * index : POOLC * (index + 1)] = dot(window, block).astype(BF)

    lat_partners = has_n.astype(jnp.int32) + has_s.astype(jnp.int32)
    pl.semaphore_wait(barrier, len(partners) + lat_partners)
    for steps in evens:
        direct(steps).start()
    forward(0, 0).start()
    loads[1].wait()
    send_lat(CTX, 0)
    send_lat(CTX, 1)
    every = slice(0, cols)
    turn_rows(ext[CTX, body].astype(F32), every, turn)
    cast_columns(turn, every, CTX)
    send_lon(CTX)
    loads[2].wait()
    turn_rows(init_ref[...].astype(F32), every, s_lon)
    cast_columns(s_lon, every, STATE)
    send_lon(STATE)

    def weights(index, part):
        channels = slice(part * hid, (part + 1) * hid)
        return jnp.concatenate([input_ref[index, tap, channels, :] for tap in range(5)], axis=0)

    def biases(index):
        gate = gbias_ref[index : index + 1]
        parts = ubias_ref[index : index + 1], gate[:, :hid], gate[:, hid:]
        return [part.reshape(1, 1, hid) for part in parts]

    def keep(stores, at, total, shape, base):
        for number, store in enumerate(stores):
            value = total[:, number * hid : (number + 1) * hid].reshape(shape)
            store[at] = value + (store[at] if base is None else base[number])

    def inputs_lon(part, e, base):
        weight = weights(0, part)
        step = near // 2

        def chunk(index, carry):
            start = index * step
            pieces = [flat(turned[e, pl.ds(start + k, step)]) for k in range(5)]
            total = dot(jnp.concatenate(pieces, axis=1), weight)
            keep((xl_z, xl_r, xl_q), pl.ds(start, step), total, (step, rows, hid), base)
            return carry

        lax.fori_loop(0, 2, chunk, 0)

    def inputs_lat(part, e, base, blocks):
        weight = weights(1, part)
        for start, size in blocks:
            pieces = [flat(ext[e, start + k : start + k + size]) for k in range(5)]
            total = dot(jnp.concatenate(pieces, axis=1), weight)
            at = slice(start, start + size)
            keep((xt_z, xt_r, xt_q), at, total, (size, cols, hid), base)

    inner = ((4, rows // 2 - 2), (rows // 2 + 2, rows // 2 - 2))
    outer = ((0, 4), (rows, 4))

    loads[3].wait()
    inputs_lat(0, CTX, biases(1), inner)
    sources = [-2, 2, 4 - 8 * parity]

    def hand_on(number):
        arrived(place(sources[number]))
        forward(number + 1, sources[number]).start()

    receive_lon(CTX)
    hand_on(0)
    hand_on(1)
    inputs_lon(0, CTX, biases(0))
    hand_on(2)
    receive_lat(CTX)
    inputs_lat(0, CTX, biases(1), outer)

    scale = chans ** (-0.5)

    def correlate(*spots):
        keys = joined_up([pool[spot] for spot in spots], 0)
        points = pool.shape[1]
        step = rows // 4

        def chunk(index, carry):
            at = pl.ds(index * step, step)
            value = lax.dot_general(
                flat(one_ref[at]), keys, (((1,), (1,)), ((), ())), preferred_element_type=F32
            )
            value = (value * scale).astype(BF)
            for number, spot in enumerate(spots):
                part = value[:, number * points : (number + 1) * points]
                corr[spot, at] = part.reshape(step, cols, points)
            return carry

        lax.fori_loop(0, 4, chunk, 0)

    loads[4].wait()
    correlate(place(0), place(2))
    if n_lon > 2 * RMAX:
        arrived(place(4 * (2 * parity - 1)))
        correlate(place(-4))
    correlate(place(-2), place(4))
    for pair in ((-1, 1), (-3, 3)):
        for steps in pair:
            arrived(place(steps))
        correlate(*[place(steps) for steps in pair])

    loads[5].wait()
    live = count_ref[0, 0]
    spots = []
    for slot in range(slots):
        offset = offset_ref[0, 0, slot]
        spots.append(jnp.where(offset < lowest, offset + n_lon, offset) - lowest)
        weight = proj_ref[class_ref[0, 0, slot]].astype(F32)
        weight = jnp.where(slot < live, weight, 0.0)
        projs[slot * weight.shape[0] : (slot + 1) * weight.shape[0]] = weight.astype(BF)

    def move(chosen):
        step = rows // 2
        wide = sum(bands[band].stop - bands[band].start for band in chosen)

        for start in range(0, rows, step):
            at = slice(start, start + step)
            pieces = []
            for spot in spots:
                parts = [corr[spot, at, bands[band]] for band in chosen]
                pieces.append(flat(joined_up(parts, 1)))
            total = dot(jnp.concatenate(pieces, axis=1), projs[...])
            moved = jnp.maximum(total, 0.0).reshape(step, wide, hid)
            done = 0
            for band in chosen:
                low, high = bands[band].start, bands[band].stop
                part = moved[:, done : done + high - low]
                done += high - low
                turn_rows(part, bands[band], turn, start)
                ext[MOT, HALO + start : HALO + start + step, bands[band]] = part.astype(BF)
        for band in chosen:
            cast_columns(turn, bands[band], MOT)

    move(edges)
    send_lon(MOT)
    move(centre)
    send_lat(MOT, 0)
    send_lat(MOT, 1)
    for steps in evens:
        direct(steps).wait_send()
    for number, source in enumerate([0] + sources):
        forward(number, source).wait_send()
    inputs_lat(1, MOT, None, inner)
    receive_lon(MOT)
    inputs_lon(1, MOT, None)
    loads[6].wait()
    loads[7].wait()

    def gates_lon(e, blocks):
        pieces = [
            joined_up([flat(turned[e, start + k : start + k + size]) for start, size in blocks], 0)
            for k in range(5)
        ]
        mixed = dot(jnp.concatenate(pieces, axis=1), zr_ref[0])
        done = 0
        for start, size in blocks:
            at = slice(start, start + size)
            shape = (size, rows, hid)
            part = mixed[done : done + size * rows]
            done += size * rows
            z_lon[at] = sigmoid(xl_z[at] + part[:, :hid].reshape(shape))
            reset = sigmoid(xl_r[at] + part[:, hid:].reshape(shape))
            low, high = max(start, 2), min(start + size, cols + 2)
            held = []
            if start < 2:
                held.append(turned[e, 2:HALO].astype(F32))
            held.append(s_lon[(low - 2) * rows : (high - 2) * rows, :].reshape(-1, rows, hid))
            if start + size > cols + 2:
                held.append(turned[e, cols + HALO : cols + HALO + 2].astype(F32))
            rs_lon[at] = (reset * joined_up(held, 0)).astype(BF)

    def update_lon(e, chosen):
        spans = [bands[band] for band in chosen]

        def take(ref, shift):
            parts = [ref[span.start + shift : span.stop + shift] for span in spans]
            return flat(joined_up(parts, 0))

        pieces = [take(rs_lon, k) for k in range(5)]
        mixed = dot(jnp.concatenate(pieces, axis=1), q_ref[0])
        candidate = jnp.tanh(take(xl_q, 2) + mixed)
        state = joined_up([s_lon[span.start * rows : span.stop * rows, :] for span in spans], 0)
        state = state + take(z_lon, 2) * (candidate - state)
        done = 0
        for span in spans:
            for column in range(span.start, span.stop):
                part = state[done * rows : (done + 1) * rows]
                s_lat[pl.ds(column, rows, stride=cols), :] = part
                done += 1
        for span in spans:
            for row in range(rows):
                part = s_lat[row * cols + span.start : row * cols + span.stop, :]
                ext[e, HALO + row, span] = part.astype(BF)

    def state_rows(spans, start, size):
        parts = [
            s_lat[row * cols + span.start : row * cols + span.stop, :]
            for row in range(start, start + size)
            for span in spans
        ]
        return joined_up(parts, 0).reshape(size, -1, hid)

    def gates_lat(e, blocks, chosen):
        spans = (slice(0, cols),) if chosen is panel else [bands[band] for band in chosen]
        wide = sum(band.stop - band.start for band in spans)

        def take(ref, lead, start, size):
            at = slice(start, start + size)
            return joined_up([ref[lead + (at, band)] for band in spans], 1)

        def put(ref, start, size, value):
            done = 0
            for band in spans:
                width = band.stop - band.start
                ref[start : start + size, band] = value[:, done : done + width]
                done += width

        pieces = [
            joined_up([flat(take(ext, (e,), start + k, size)) for start, size in blocks], 0)
            for k in range(5)
        ]
        mixed = dot(jnp.concatenate(pieces, axis=1), zr_ref[1])
        done = 0
        for start, size in blocks:
            shape = (size, wide, hid)
            part = mixed[done : done + size * wide]
            done += size * wide
            z = sigmoid(take(xt_z, (), start, size) + part[:, :hid].reshape(shape))
            put(z_lat, start, size, z)
            reset = sigmoid(take(xt_r, (), start, size) + part[:, hid:].reshape(shape))
            if start == 0:
                held = [take(ext, (e,), 2, 2).astype(F32), state_rows(spans, 0, 2)]
            elif start + size == rows + 4:
                held = [state_rows(spans, rows - 2, 2), take(ext, (e,), rows + HALO, 2).astype(F32)]
            else:
                held = [state_rows(spans, start - 2, size)]
            put(rs_lat, start, size, (reset * joined_up(held, 0)).astype(BF))

    def update_lat(e, chosen, blocks):
        spans = (slice(0, cols),) if chosen is panel else [bands[band] for band in chosen]
        wide = sum(span.stop - span.start for span in spans)

        def take(ref, start, size):
            return joined_up([ref[start : start + size, span] for span in spans], 1)

        def rows_of(ref, shift):
            parts = [flat(take(ref, start + shift, size)) for start, size in blocks]
            return joined_up(parts, 0)

        pieces = [rows_of(rs_lat, k) for k in range(5)]
        mixed = dot(jnp.concatenate(pieces, axis=1), q_ref[1])
        done = 0
        for start, size in blocks:
            shape = (size, wide, hid)
            part = mixed[done : done + size * wide].reshape(shape)
            done += size * wide
            candidate = jnp.tanh(take(xt_q, start + 2, size) + part)
            state = state_rows(spans, start, size)
            state = state + take(z_lat, start + 2, size) * (candidate - state)
            column = 0
            for span in spans:
                width = span.stop - span.start
                value = state[:, column : column + width]
                out_ref[start : start + size, span] = value
                turn_rows(value, span, s_lon, start)
                column += width

    def cast_bands(e, chosen):
        for band in chosen:
            cast_columns(s_lon, bands[band], e)

    rim = ((0, HALO), (rows - HALO, HALO))

    def iteration(index, carry):
        e = STATE + index
        gates_lon(e, ((4, cols - 4),))
        receive_lon(e)
        gates_lon(e, ((0, 4), (cols, 4)))
        update_lon(e, edges)
        send_lat(e, 0, edges)
        send_lat(e, 1, edges)
        update_lon(e, centre)
        send_lat(e, 0, centre)
        send_lat(e, 1, centre)

        @pl.when(index == 0)
        def _():
            receive_lat(MOT)
            inputs_lat(1, MOT, None, outer)

        gates_lat(e, ((4, rows - 4),), panel)
        update_lat(e, panel, ((HALO, rows - 2 * HALO),))
        receive_lat(e, edges)
        gates_lat(e, outer, edges)
        update_lat(e, edges, rim)
        cast_bands(e + 1, edges)

        @pl.when(index < ITERS - 1)
        def _():
            send_lon(e + 1)

        receive_lat(e, centre)
        gates_lat(e, outer, centre)
        update_lat(e, centre, rim)
        cast_bands(e + 1, centre)
        return carry

    lax.fori_loop(0, ITERS, iteration, 0)


def local(
    n_lat,
    n_lon,
    feat_one,
    feat_two,
    context_in,
    hidden_init,
    corr_proj,
    input_conv,
    state_zr,
    state_q,
    update_bias,
    gate_bias,
    blk_offset,
    blk_class,
    blk_count,
):
    rows, cols, chans = feat_one.shape
    hid = hidden_init.shape[2]
    points = POOLR * POOLC
    slots = blk_offset.shape[2]
    reach = min(n_lon, 2 * RMAX + 1)
    near = cols + 4
    tall = rows + 2 * HALO
    count = STATE + ITERS
    taps = state_zr.shape[1]
    state_zr = state_zr.reshape(2, taps * hid, 2 * hid)
    state_q = state_q.reshape(2, taps * hid, hid)
    vmem = pl.BlockSpec(memory_space=pltpu.VMEM)
    smem = pl.BlockSpec(memory_space=pltpu.SMEM)
    hbm = pl.BlockSpec(memory_space=pl.ANY)
    held = (feat_one, feat_two, hidden_init, corr_proj, input_conv, state_zr, state_q)
    hidden = pl.pallas_call(
        functools.partial(kernel, n_lat, n_lon),
        out_shape=jax.ShapeDtypeStruct((rows, cols, hid), F32),
        in_specs=[smem] * 3 + [hbm] * 8 + [vmem] * 2,
        out_specs=vmem,
        scratch_shapes=[pltpu.VMEM(value.shape, BF) for value in held]
        + [
            pltpu.VMEM((count, tall, cols, hid), BF),
            pltpu.VMEM((count + 1, cols + 2 * HALO, rows, hid), BF),
            pltpu.VMEM((reach, points, chans), BF),
            pltpu.VMEM((reach, rows, cols, points), BF),
            pltpu.VMEM((slots * points, hid), BF),
            pltpu.VMEM((cols * rows, hid), F32),
            pltpu.VMEM((near, rows, hid), F32),
            pltpu.VMEM((near, rows, hid), F32),
            pltpu.VMEM((near, rows, hid), F32),
            pltpu.VMEM((rows + 4, cols, hid), F32),
            pltpu.VMEM((rows + 4, cols, hid), F32),
            pltpu.VMEM((rows + 4, cols, hid), F32),
            pltpu.VMEM((cols * rows, hid), F32),
            pltpu.VMEM((rows * cols, hid), F32),
            pltpu.VMEM((near, rows, hid), BF),
            pltpu.VMEM((rows + 4, cols, hid), BF),
            pltpu.VMEM((near, rows, hid), F32),
            pltpu.VMEM((rows + 4, cols, hid), F32),
            pltpu.SemaphoreType.DMA((8,)),
            pltpu.SemaphoreType.DMA((count, 2, 3)),
            pltpu.SemaphoreType.DMA((count, 2, 3)),
            pltpu.SemaphoreType.DMA((count, 2)),
            pltpu.SemaphoreType.DMA((count, 2)),
            pltpu.SemaphoreType.DMA((4,)),
            pltpu.SemaphoreType.DMA((reach,)),
            pltpu.SemaphoreType.DMA((4,)),
        ],
        compiler_params=pltpu.CompilerParams(
            collective_id=0, has_side_effects=True, vmem_limit_bytes=56 * 1024 * 1024
        ),
        name="refine",
    )(
        blk_offset,
        blk_class,
        blk_count,
        feat_one,
        feat_two,
        context_in,
        hidden_init,
        corr_proj,
        input_conv,
        state_zr,
        state_q,
        update_bias,
        gate_bias,
    )
    return hidden.astype(BF)


def solution(mesh):
    placed = (
        P("lat", "lon", None),
        P("lat", "lon", None),
        P("lat", "lon", None),
        P("lat", "lon", None),
        P(),
        P(),
        P(),
        P(),
        P(),
        P(),
        P("lat", "lon", None),
        P("lat", "lon", None),
        P("lat", "lon"),
    )
    return jax.shard_map(
        functools.partial(local, mesh.shape["lat"], mesh.shape["lon"]),
        mesh=mesh,
        in_specs=placed,
        out_specs=P("lat", "lon", None),
        check_vma=False,
    )
```

```python
import functools

import jax
import jax.numpy as jnp
from jax import lax
from jax.experimental import pallas as pl
from jax.experimental.pallas import tpu as pltpu
from jax.sharding import PartitionSpec as P

POOLR = 8
POOLC = 16
RMAX = 4
ITERS = 4
HALO = 4
CTX, MOT, STATE = 0, 1, 2
MESH = pl.DeviceIdType.MESH
BF = jnp.bfloat16
F32 = jnp.float32


def sigmoid(value):
    return 0.5 * jnp.tanh(0.5 * value) + 0.5


def dot(left, right):
    return jnp.dot(left, right, preferred_element_type=F32)


def flat(value):
    return value.reshape(-1, value.shape[-1])


def joined_up(parts, axis):
    return parts[0] if len(parts) == 1 else jnp.concatenate(parts, axis=axis)


def kernel(
    n_lat,
    n_lon,
    offset_ref,
    class_ref,
    count_ref,
    one_hbm,
    two_hbm,
    ctx_hbm,
    init_hbm,
    proj_hbm,
    input_hbm,
    zr_hbm,
    q_hbm,
    ubias_ref,
    gbias_ref,
    out_ref,
    one_ref,
    two_ref,
    init_ref,
    proj_ref,
    input_ref,
    zr_ref,
    q_ref,
    ext,
    turned,
    pool,
    corr,
    projs,
    turn,
    xl_z,
    xl_r,
    xl_q,
    xt_z,
    xt_r,
    xt_q,
    s_lon,
    s_lat,
    rs_lon,
    rs_lat,
    z_lon,
    z_lat,
    load_sem,
    ns_send,
    ns_recv,
    ew_send,
    ew_recv,
    pool_send,
    pool_recv,
    pass_send,
):
    rows, cols, chans = one_ref.shape
    hid = init_ref.shape[2]
    near = cols + 4
    slots = offset_ref.shape[2]
    lat, lon = lax.axis_index("lat"), lax.axis_index("lon")
    north, south = lax.rem(lat + n_lat - 1, n_lat), lax.rem(lat + 1, n_lat)
    west, east = lax.rem(lon + n_lon - 1, n_lon), lax.rem(lon + 1, n_lon)
    has_n, has_s = lat > 0, lat < n_lat - 1
    parity = lax.rem(lon, 2)
    lowest = -min(RMAX, (n_lon - 1) // 2)
    highest = min(RMAX, n_lon // 2)

    top = slice(HALO, 2 * HALO)
    bottom = slice(rows, rows + HALO)
    above = slice(0, HALO)
    below = slice(rows + HALO, rows + 2 * HALO)
    body = slice(HALO, HALO + rows)

    loads = [
        pltpu.make_async_copy(source, target, load_sem.at[number])
        for number, (source, target) in enumerate(
            (
                (two_hbm, two_ref),
                (ctx_hbm, ext.at[CTX, body]),
                (init_hbm, init_ref),
                (input_hbm, input_ref),
                (one_hbm, one_ref),
                (proj_hbm, proj_ref),
                (zr_hbm, zr_ref),
                (q_hbm, q_ref),
            )
        )
    ]
    for load in loads:
        load.start()

    def place(offset):
        return lax.rem(offset - lowest + n_lon, n_lon)

    def along(steps):
        return lax.rem(lon + steps + n_lon, n_lon)

    evens = [d for d in (2, -2, 4, -4) if lowest <= d <= highest]

    barrier = pltpu.get_barrier_semaphore()
    partners = [1, -1] + evens
    for steps in partners:
        pl.semaphore_signal(
            barrier, inc=1, device_id=(lat, along(steps)), device_id_type=MESH
        )

    @pl.when(has_n)
    def _():
        pl.semaphore_signal(barrier, inc=1, device_id=(north, lon), device_id_type=MESH)

    @pl.when(has_s)
    def _():
        pl.semaphore_signal(barrier, inc=1, device_id=(south, lon), device_id_type=MESH)

    left, right = slice(0, 16), slice(cols - 16, cols)
    bands = (left, right, slice(16, cols - 16))
    edges, centre, panel = (0, 1), (2,), (0, 1, 2)

    def to_lat(e, way, band):
        return pltpu.make_async_remote_copy(
            src_ref=ext.at[e, bottom if way else top, bands[band]],
            dst_ref=ext.at[e, above if way else below, bands[band]],
            send_sem=ns_send.at[e, way, band],
            recv_sem=ns_recv.at[e, way, band],
            device_id=(south if way else north, lon),
            device_id_type=MESH,
        )

    def to_lon(e, way):
        return pltpu.make_async_remote_copy(
            src_ref=turned.at[e, cols : cols + HALO] if way else turned.at[e, HALO : 2 * HALO],
            dst_ref=turned.at[e, 0:HALO] if way else turned.at[e, cols + HALO :],
            send_sem=ew_send.at[e, way],
            recv_sem=ew_recv.at[e, way],
            device_id=(lat, east if way else west),
            device_id_type=MESH,
        )

    def send_lat(e, way, chosen=panel):
        @pl.when(has_s if way else has_n)
        def _():
            for band in chosen:
                to_lat(e, way, band).start()

    def receive_lat(e, chosen=panel):
        @pl.when(has_s)
        def _():
            for band in chosen:
                to_lat(e, 0, band).wait_recv()
                to_lat(e, 1, band).wait_send()

        @pl.when(has_n)
        def _():
            for band in chosen:
                to_lat(e, 1, band).wait_recv()
                to_lat(e, 0, band).wait_send()

    @pl.when(jnp.logical_not(has_s))
    def _():
        for e in range(ext.shape[0]):
            ext[e, below] = jnp.zeros((HALO, cols, hid), BF)

    @pl.when(jnp.logical_not(has_n))
    def _():
        for e in range(ext.shape[0]):
            ext[e, above] = jnp.zeros((HALO, cols, hid), BF)

    def send_lon(e):
        for way in range(2):
            to_lon(e, way).start()

    def receive_lon(e):
        for way in range(2):
            to_lon(e, way).wait()

    def turn_rows(value, band, target, first=0):
        low, high = band.start, band.stop
        for row in range(value.shape[0]):
            target[pl.ds(low * rows + first + row, high - low, stride=rows), :] = value[row]

    def cast_columns(source, band, e):
        low, high = band.start, band.stop
        value = source[low * rows : high * rows, :].astype(BF).reshape(high - low, rows, hid)
        turned[e, HALO + low : HALO + high] = value

    def direct(steps):
        return pltpu.make_async_remote_copy(
            src_ref=pool.at[-lowest],
            dst_ref=pool.at[place(-steps)],
            send_sem=pool_send.at[evens.index(steps)],
            recv_sem=pool_recv.at[place(-steps)],
            device_id=(lat, along(steps)),
            device_id_type=MESH,
        )

    sibling = lon + 1 - 2 * parity

    def forward(number, source):
        target = source - 1 + 2 * parity
        return pltpu.make_async_remote_copy(
            src_ref=pool.at[place(source)],
            dst_ref=pool.at[place(target)],
            send_sem=pass_send.at[number],
            recv_sem=pool_recv.at[place(target)],
            device_id=(lat, sibling),
            device_id_type=MESH,
        )

    def arrived(spot):
        return pltpu.make_async_remote_copy(
            src_ref=pool.at[-lowest],
            dst_ref=pool.at[spot],
            send_sem=pool_send.at[0],
            recv_sem=pool_recv.at[spot],
            device_id=(lat, sibling),
            device_id_type=MESH,
        ).wait_recv()

    point = lax.broadcasted_iota(jnp.int32, (POOLC, 2 * cols), 0)
    cell = lax.rem(lax.broadcasted_iota(jnp.int32, (POOLC, 2 * cols), 1), cols)
    pool_rows, pool_cols = rows // POOLR, cols // POOLC
    inside = (cell >= point * pool_cols) & (cell < (point + 1) * pool_cols)
    window = jnp.where(inside, 1.0 / (pool_rows * pool_cols), 0.0).astype(BF)
    loads[0].wait()
    for index in range(POOLR):
        block = flat(two_ref[pool_rows * index : pool_rows * (index + 1)])
        pool[-lowest, POOLC * index : POOLC * (index + 1)] = dot(window, block).astype(BF)

    lat_partners = has_n.astype(jnp.int32) + has_s.astype(jnp.int32)
    pl.semaphore_wait(barrier, len(partners) + lat_partners)
    for steps in evens:
        direct(steps).start()
    forward(0, 0).start()
    loads[1].wait()
    send_lat(CTX, 0)
    send_lat(CTX, 1)
    every = slice(0, cols)
    turn_rows(ext[CTX, body].astype(F32), every, turn)
    cast_columns(turn, every, CTX)
    send_lon(CTX)
    loads[2].wait()
    turn_rows(init_ref[...].astype(F32), every, s_lon)
    cast_columns(s_lon, every, STATE)
    send_lon(STATE)

    def weights(index, part):
        channels = slice(part * hid, (part + 1) * hid)
        return jnp.concatenate([input_ref[index, tap, channels, :] for tap in range(5)], axis=0)

    def biases(index):
        gate = gbias_ref[index : index + 1]
        parts = ubias_ref[index : index + 1], gate[:, :hid], gate[:, hid:]
        return [part.reshape(1, 1, hid) for part in parts]

    def keep(stores, at, total, shape, base):
        for number, store in enumerate(stores):
            value = total[:, number * hid : (number + 1) * hid].reshape(shape)
            store[at] = value + (store[at] if base is None else base[number])

    def inputs_lon(part, e, base):
        weight = weights(0, part)
        step = near // 2

        def chunk(index, carry):
            start = index * step
            pieces = [flat(turned[e, pl.ds(start + k, step)]) for k in range(5)]
            total = dot(jnp.concatenate(pieces, axis=1), weight)
            keep((xl_z, xl_r, xl_q), pl.ds(start, step), total, (step, rows, hid), base)
            return carry

        lax.fori_loop(0, 2, chunk, 0)

    def inputs_lat(part, e, base, blocks):
        weight = weights(1, part)
        for start, size in blocks:
            pieces = [flat(ext[e, start + k : start + k + size]) for k in range(5)]
            total = dot(jnp.concatenate(pieces, axis=1), weight)
            at = slice(start, start + size)
            keep((xt_z, xt_r, xt_q), at, total, (size, cols, hid), base)

    inner = ((4, rows // 2 - 2), (rows // 2 + 2, rows // 2 - 2))
    outer = ((0, 4), (rows, 4))

    loads[3].wait()
    inputs_lat(0, CTX, biases(1), inner)
    sources = [-2, 2, 4 - 8 * parity]

    def hand_on(number):
        arrived(place(sources[number]))
        forward(number + 1, sources[number]).start()

    receive_lon(CTX)
    hand_on(0)
    hand_on(1)
    inputs_lon(0, CTX, biases(0))
    hand_on(2)
    receive_lat(CTX)
    inputs_lat(0, CTX, biases(1), outer)

    scale = chans ** (-0.5)

    def correlate(*spots):
        keys = joined_up([pool[spot] for spot in spots], 0)
        points = pool.shape[1]
        step = rows // 4

        def chunk(index, carry):
            at = pl.ds(index * step, step)
            value = lax.dot_general(
                flat(one_ref[at]), keys, (((1,), (1,)), ((), ())), preferred_element_type=F32
            )
            value = (value * scale).astype(BF)
            for number, spot in enumerate(spots):
                part = value[:, number * points : (number + 1) * points]
                corr[spot, at] = part.reshape(step, cols, points)
            return carry

        lax.fori_loop(0, 4, chunk, 0)

    loads[4].wait()
    correlate(place(0), place(2))
    if n_lon > 2 * RMAX:
        arrived(place(4 * (2 * parity - 1)))
        correlate(place(-4))
    correlate(place(-2), place(4))
    for pair in ((-1, 1), (-3, 3)):
        for steps in pair:
            arrived(place(steps))
        correlate(*[place(steps) for steps in pair])

    loads[5].wait()
    live = count_ref[0, 0]
    spots = []
    for slot in range(slots):
        offset = offset_ref[0, 0, slot]
        spots.append(jnp.where(offset < lowest, offset + n_lon, offset) - lowest)
        weight = proj_ref[class_ref[0, 0, slot]].astype(F32)
        weight = jnp.where(slot < live, weight, 0.0)
        projs[slot * weight.shape[0] : (slot + 1) * weight.shape[0]] = weight.astype(BF)

    def move(chosen):
        step = rows // 2
        wide = sum(bands[band].stop - bands[band].start for band in chosen)

        for start in range(0, rows, step):
            at = slice(start, start + step)
            pieces = []
            for spot in spots:
                parts = [corr[spot, at, bands[band]] for band in chosen]
                pieces.append(flat(joined_up(parts, 1)))
            total = dot(jnp.concatenate(pieces, axis=1), projs[...])
            moved = jnp.maximum(total, 0.0).reshape(step, wide, hid)
            done = 0
            for band in chosen:
                low, high = bands[band].start, bands[band].stop
                part = moved[:, done : done + high - low]
                done += high - low
                turn_rows(part, bands[band], turn, start)
                ext[MOT, HALO + start : HALO + start + step, bands[band]] = part.astype(BF)
        for band in chosen:
            cast_columns(turn, bands[band], MOT)

    move(edges)
    send_lon(MOT)
    move(centre)
    send_lat(MOT, 0)
    send_lat(MOT, 1)
    for steps in evens:
        direct(steps).wait_send()
    for number, source in enumerate([0] + sources):
        forward(number, source).wait_send()
    inputs_lat(1, MOT, None, inner)
    receive_lon(MOT)
    inputs_lon(1, MOT, None)
    loads[6].wait()
    loads[7].wait()

    def gates_lon(e, blocks):
        pieces = [
            joined_up([flat(turned[e, start + k : start + k + size]) for start, size in blocks], 0)
            for k in range(5)
        ]
        mixed = dot(jnp.concatenate(pieces, axis=1), zr_ref[0])
        done = 0
        for start, size in blocks:
            at = slice(start, start + size)
            shape = (size, rows, hid)
            part = mixed[done : done + size * rows]
            done += size * rows
            z_lon[at] = sigmoid(xl_z[at] + part[:, :hid].reshape(shape))
            reset = sigmoid(xl_r[at] + part[:, hid:].reshape(shape))
            low, high = max(start, 2), min(start + size, cols + 2)
            held = []
            if start < 2:
                held.append(turned[e, 2:HALO].astype(F32))
            held.append(s_lon[(low - 2) * rows : (high - 2) * rows, :].reshape(-1, rows, hid))
            if start + size > cols + 2:
                held.append(turned[e, cols + HALO : cols + HALO + 2].astype(F32))
            rs_lon[at] = (reset * joined_up(held, 0)).astype(BF)

    def update_lon(spans):
        def take(ref, shift):
            parts = [ref[span.start + shift : span.stop + shift] for span in spans]
            return flat(joined_up(parts, 0))

        pieces = [take(rs_lon, k) for k in range(5)]
        mixed = dot(jnp.concatenate(pieces, axis=1), q_ref[0])
        candidate = jnp.tanh(take(xl_q, 2) + mixed)
        state = joined_up([s_lon[span.start * rows : span.stop * rows, :] for span in spans], 0)
        state = state + take(z_lon, 2) * (candidate - state)
        done = 0
        for span in spans:
            for column in range(span.start, span.stop):
                part = state[done * rows : (done + 1) * rows]
                s_lat[pl.ds(column, rows, stride=cols), :] = part
                done += 1

    def cast_rows(e, chosen):
        for band in chosen:
            span = bands[band]
            for row in range(rows):
                part = s_lat[row * cols + span.start : row * cols + span.stop, :]
                ext[e, HALO + row, span] = part.astype(BF)

    def state_rows(spans, start, size):
        parts = [
            s_lat[row * cols + span.start : row * cols + span.stop, :]
            for row in range(start, start + size)
            for span in spans
        ]
        return joined_up(parts, 0).reshape(size, -1, hid)

    def gates_lat(e, blocks, chosen):
        spans = (slice(0, cols),) if chosen is panel else [bands[band] for band in chosen]
        wide = sum(band.stop - band.start for band in spans)

        def take(ref, lead, start, size):
            at = slice(start, start + size)
            return joined_up([ref[lead + (at, band)] for band in spans], 1)

        def put(ref, start, size, value):
            done = 0
            for band in spans:
                width = band.stop - band.start
                ref[start : start + size, band] = value[:, done : done + width]
                done += width

        pieces = [
            joined_up([flat(take(ext, (e,), start + k, size)) for start, size in blocks], 0)
            for k in range(5)
        ]
        mixed = dot(jnp.concatenate(pieces, axis=1), zr_ref[1])
        done = 0
        for start, size in blocks:
            shape = (size, wide, hid)
            part = mixed[done : done + size * wide]
            done += size * wide
            z = sigmoid(take(xt_z, (), start, size) + part[:, :hid].reshape(shape))
            put(z_lat, start, size, z)
            reset = sigmoid(take(xt_r, (), start, size) + part[:, hid:].reshape(shape))
            if start == 0:
                held = [take(ext, (e,), 2, 2).astype(F32), state_rows(spans, 0, 2)]
            elif start + size == rows + 4:
                held = [state_rows(spans, rows - 2, 2), take(ext, (e,), rows + HALO, 2).astype(F32)]
            else:
                held = [state_rows(spans, start - 2, size)]
            put(rs_lat, start, size, (reset * joined_up(held, 0)).astype(BF))

    def update_lat(e, chosen, blocks):
        spans = (slice(0, cols),) if chosen is panel else [bands[band] for band in chosen]
        wide = sum(span.stop - span.start for span in spans)

        def take(ref, start, size):
            return joined_up([ref[start : start + size, span] for span in spans], 1)

        def rows_of(ref, shift):
            parts = [flat(take(ref, start + shift, size)) for start, size in blocks]
            return joined_up(parts, 0)

        pieces = [rows_of(rs_lat, k) for k in range(5)]
        mixed = dot(jnp.concatenate(pieces, axis=1), q_ref[1])
        done = 0
        for start, size in blocks:
            shape = (size, wide, hid)
            part = mixed[done : done + size * wide].reshape(shape)
            done += size * wide
            candidate = jnp.tanh(take(xt_q, start + 2, size) + part)
            state = state_rows(spans, start, size)
            state = state + take(z_lat, start + 2, size) * (candidate - state)
            column = 0
            for span in spans:
                width = span.stop - span.start
                value = state[:, column : column + width]
                out_ref[start : start + size, span] = value
                turn_rows(value, span, s_lon, start)
                column += width

    def cast_bands(e, chosen):
        for band in chosen:
            cast_columns(s_lon, bands[band], e)

    rim = ((0, HALO), (rows - HALO, HALO))

    def iteration(index, carry):
        e = STATE + index
        gates_lon(e, ((4, cols - 4),))
        update_lon([slice(HALO, cols - HALO)])
        cast_rows(e, centre)
        send_lat(e, 0, centre)
        send_lat(e, 1, centre)
        receive_lon(e)
        gates_lon(e, ((0, 4), (cols, 4)))
        update_lon([slice(0, HALO), slice(cols - HALO, cols)])
        cast_rows(e, edges)
        send_lat(e, 0, edges)
        send_lat(e, 1, edges)

        @pl.when(index == 0)
        def _():
            receive_lat(MOT)
            inputs_lat(1, MOT, None, outer)

        gates_lat(e, ((4, rows - 4),), panel)
        update_lat(e, panel, ((HALO, rows - 2 * HALO),))
        receive_lat(e, edges)
        gates_lat(e, outer, edges)
        update_lat(e, edges, rim)
        cast_bands(e + 1, edges)

        @pl.when(index < ITERS - 1)
        def _():
            send_lon(e + 1)

        receive_lat(e, centre)
        gates_lat(e, outer, centre)
        update_lat(e, centre, rim)
        cast_bands(e + 1, centre)
        return carry

    lax.fori_loop(0, ITERS, iteration, 0)


def local(
    n_lat,
    n_lon,
    feat_one,
    feat_two,
    context_in,
    hidden_init,
    corr_proj,
    input_conv,
    state_zr,
    state_q,
    update_bias,
    gate_bias,
    blk_offset,
    blk_class,
    blk_count,
):
    rows, cols, chans = feat_one.shape
    hid = hidden_init.shape[2]
    points = POOLR * POOLC
    slots = blk_offset.shape[2]
    reach = min(n_lon, 2 * RMAX + 1)
    near = cols + 4
    tall = rows + 2 * HALO
    count = STATE + ITERS
    taps = state_zr.shape[1]
    state_zr = state_zr.reshape(2, taps * hid, 2 * hid)
    state_q = state_q.reshape(2, taps * hid, hid)
    vmem = pl.BlockSpec(memory_space=pltpu.VMEM)
    smem = pl.BlockSpec(memory_space=pltpu.SMEM)
    hbm = pl.BlockSpec(memory_space=pl.ANY)
    held = (feat_one, feat_two, hidden_init, corr_proj, input_conv, state_zr, state_q)
    hidden = pl.pallas_call(
        functools.partial(kernel, n_lat, n_lon),
        out_shape=jax.ShapeDtypeStruct((rows, cols, hid), F32),
        in_specs=[smem] * 3 + [hbm] * 8 + [vmem] * 2,
        out_specs=vmem,
        scratch_shapes=[pltpu.VMEM(value.shape, BF) for value in held]
        + [
            pltpu.VMEM((count, tall, cols, hid), BF),
            pltpu.VMEM((count + 1, cols + 2 * HALO, rows, hid), BF),
            pltpu.VMEM((reach, points, chans), BF),
            pltpu.VMEM((reach, rows, cols, points), BF),
            pltpu.VMEM((slots * points, hid), BF),
            pltpu.VMEM((cols * rows, hid), F32),
            pltpu.VMEM((near, rows, hid), F32),
            pltpu.VMEM((near, rows, hid), F32),
            pltpu.VMEM((near, rows, hid), F32),
            pltpu.VMEM((rows + 4, cols, hid), F32),
            pltpu.VMEM((rows + 4, cols, hid), F32),
            pltpu.VMEM((rows + 4, cols, hid), F32),
            pltpu.VMEM((cols * rows, hid), F32),
            pltpu.VMEM((rows * cols, hid), F32),
            pltpu.VMEM((near, rows, hid), BF),
            pltpu.VMEM((rows + 4, cols, hid), BF),
            pltpu.VMEM((near, rows, hid), F32),
            pltpu.VMEM((rows + 4, cols, hid), F32),
            pltpu.SemaphoreType.DMA((8,)),
            pltpu.SemaphoreType.DMA((count, 2, 3)),
            pltpu.SemaphoreType.DMA((count, 2, 3)),
            pltpu.SemaphoreType.DMA((count, 2)),
            pltpu.SemaphoreType.DMA((count, 2)),
            pltpu.SemaphoreType.DMA((4,)),
            pltpu.SemaphoreType.DMA((reach,)),
            pltpu.SemaphoreType.DMA((4,)),
        ],
        compiler_params=pltpu.CompilerParams(
            collective_id=0, has_side_effects=True, vmem_limit_bytes=56 * 1024 * 1024
        ),
        name="refine",
    )(
        blk_offset,
        blk_class,
        blk_count,
        feat_one,
        feat_two,
        context_in,
        hidden_init,
        corr_proj,
        input_conv,
        state_zr,
        state_q,
        update_bias,
        gate_bias,
    )
    return hidden.astype(BF)


def solution(mesh):
    placed = (
        P("lat", "lon", None),
        P("lat", "lon", None),
        P("lat", "lon", None),
        P("lat", "lon", None),
        P(),
        P(),
        P(),
        P(),
        P(),
        P(),
        P("lat", "lon", None),
        P("lat", "lon", None),
        P("lat", "lon"),
    )
    return jax.shard_map(
        functools.partial(local, mesh.shape["lat"], mesh.shape["lon"]),
        mesh=mesh,
        in_specs=placed,
        out_specs=P("lat", "lon", None),
        check_vma=False,
    )
```
